32 devices in a mesh: space: 4 (over y, x), vel: 8 (over z, core).
Axes of the slice: x: 2, y: 2, z: 4, core: 2. Of those that a mesh axis runs over, the one named last changes fastest.
Arguments:
- distribution: float32 [4, 16, 16, 32768], P('space', None, None, 'vel'), may hold values from 0.003 to 450, as said below
- inflow: float32 [2, 16, 16, 32768], P(None, None, None, 'vel'), may hold values from 0.3 to 3
- wall_temp: float32 [2, 16, 16], replicated, may hold values from 0.5 to 4
- face_type: int32 [2, 16, 16], replicated, may hold values from 0 to 2
Outputs:
- updated: float32 [4, 16, 16, 32768], P('space', None, None, 'vel')
- fields: float32 [8, 4, 16, 16], P(None, 'space')
The draws below stay inside these ranges and needn't reach their ends.
Inputs may be any that keep to these rules, and one draw needn't show every extreme that they name: `distribution`: every entry is positive.
All inputs are finite; a program needn't handle non-finite values.
Results may differ from the reference program's by a relative error of at most 0.0003.
Values sent between devices are 32-bit elements; how exact they have to be, the bound alone decides.
A program may use at most 128 MiB of HBM per device.

```python
import math
import jax
import jax.numpy as jnp

NY = 16
NZ = 16
NVX = 32
NVY = 32
NVZ = 32
OUTER = 2
INNER = 3
NX = 4
NV = 32768
VEL_DEV = 4096
N_VEL = 8


def plume_speeds():
    velocity_total = NVX * NVY * NVZ
    velocity_index = jnp.arange(velocity_total, dtype=jnp.int32)
    halves = VEL_DEV // 2
    owner_shard = velocity_index // VEL_DEV
    within = velocity_index % VEL_DEV
    upper_half = within // halves
    ranked = owner_shard * halves + within % halves
    layer_size = NVY * NVZ
    level_x = ranked // layer_size
    remain = ranked % layer_size
    across_y = remain // NVZ
    across_z = remain % NVZ
    sign_x = 2.0 * upper_half.astype(jnp.float32) - 1.0
    speed_x = sign_x * (level_x.astype(jnp.float32) + 0.5) * (8.0 / NVX)
    speed_y = (across_y.astype(jnp.float32) + 0.5) * (8.0 / NVY) - 4.0
    speed_z = (across_z.astype(jnp.float32) + 0.5) * (8.0 / NVZ) - 4.0
    return (speed_x, speed_y, speed_z)


def gas_profile(speeds, drift, temp_cell):
    offset_x = speeds[0] - drift[0]
    offset_y = speeds[1] - drift[1]
    offset_z = speeds[2] - drift[2]
    squared = offset_x * offset_x + offset_y * offset_y + offset_z * offset_z
    return 512.0 * jnp.exp(-squared / (2.0 * temp_cell)) / (2.0 * jnp.pi * temp_cell) ** 1.5


def draw_distribution(key, part):
    speeds = plume_speeds()
    cell_shape = (NX, NY, NZ, 1)
    density_key = jax.random.fold_in(key, 21)
    core_key = jax.random.fold_in(key, 22)
    beam_key = jax.random.fold_in(key, 23)
    weight_key = jax.random.fold_in(key, 24)
    core_temp_key = jax.random.fold_in(key, 25)
    beam_temp_key = jax.random.fold_in(key, 26)
    noise_key = jax.random.fold_in(key, 27)
    particle_concentration = jnp.exp(jax.random.uniform(density_key, cell_shape, jnp.float32, jnp.log(0.3), jnp.log(3.0)))
    core_local = jax.random.uniform(core_key, (3,) + cell_shape, jnp.float32, -1.0, 1.0)
    beam_local = jax.random.uniform(beam_key, (3,) + cell_shape, jnp.float32, -1.5, 1.5)
    core_drift = [core_local[index] for index in range(3)]
    beam_drift = [core_local[index] + beam_local[index] for index in range(3)]
    beam_weight = jax.random.uniform(weight_key, cell_shape, jnp.float32, 0.1, 0.35)
    core_temp = jnp.exp(jax.random.uniform(core_temp_key, cell_shape, jnp.float32, jnp.log(0.6), jnp.log(1.5)))
    beam_temp = jnp.exp(jax.random.uniform(beam_temp_key, cell_shape, jnp.float32, jnp.log(0.6), jnp.log(1.5)))
    noise = jnp.exp(jax.random.uniform(noise_key, (NX, NY, NZ, NV), jnp.float32, jnp.log(0.5), jnp.log(2.0)))
    mixture = (1.0 - beam_weight) * gas_profile(speeds, core_drift, core_temp) + beam_weight * gas_profile(speeds, beam_drift, beam_temp)
    return particle_concentration * noise * (mixture + 0.02)


def touch_ends(drawn, key, least, largest):
    shape = drawn.shape
    spot = [jax.random.randint(jax.random.fold_in(key, axis), (), 0, shape[axis]) for axis in range(len(shape))]
    drawn = drawn.at[tuple(spot)].set(least)
    longest = shape.index(max(shape))
    spot[longest] = (spot[longest] + 1) % shape[longest]
    return drawn.at[tuple(spot)].set(largest)


def block_levels(key, shape, pieces, low, high):
    gain = 1.0
    for position, shards_of in pieces:
        steps = jax.random.uniform(jax.random.fold_in(jax.random.fold_in(key, 6), position), (shards_of,), jnp.float32, low / len(pieces), high / len(pieces))
        gain = gain * jnp.repeat(jnp.exp(steps), shape[position] // shards_of).reshape((-1,) + (1,) * (len(shape) - 1 - position))
    return gain


def setup_inputs(seed: int = 0) -> dict:
    keys = jax.random.split(jax.random.key(seed), 5)
    distribution = draw_distribution(jax.random.fold_in(keys[4], 71), 0)
    inflow = jnp.clip(jnp.exp(math.log(3.0) - 2.3025851 * jax.random.uniform(keys[1], (2, NY, NZ, NV), jnp.float32) ** block_levels(keys[1], (2, NY, NZ, NV), ((3, 8),), -0.2, 0.2)), 0.3, 3.0)
    wall_temp = jnp.clip(jnp.exp(jax.random.uniform(keys[2], (2, NY, NZ), jnp.float32, math.log(0.5), math.log(4.0))), 0.5, 4.0)
    face_type = touch_ends(jax.random.randint(keys[3], (2, NY, NZ), 0, 3), jax.random.fold_in(keys[3], 1), 0, 2).astype(jnp.int32)
    return {"distribution": distribution, "inflow": inflow, "wall_temp": wall_temp, "face_type": face_type}


box_volume = 512.0
speed_top = 4.0
courant = 0.08
impact_rate_field = 0.8
shakhov_factor = 1.0 / 3.0


def velocity_table(count_x, count_y, count_z, shards):
    velocity_total = count_x * count_y * count_z
    velocity_index = jnp.arange(velocity_total, dtype=jnp.int32)
    per_shard = velocity_total // shards
    halves = per_shard // 2
    owner_shard = velocity_index // per_shard
    within = velocity_index % per_shard
    upper_half = within // halves
    ranked = owner_shard * halves + within % halves
    layer_size = count_y * count_z
    level_x = ranked // layer_size
    remain = ranked % layer_size
    across_y = remain // count_z
    across_z = remain % count_z
    sign_x = 2.0 * upper_half.astype(jnp.float32) - 1.0
    speed_x = sign_x * (level_x.astype(jnp.float32) + 0.5) * (2.0 * speed_top / count_x)
    speed_y = (across_y.astype(jnp.float32) + 0.5) * (2.0 * speed_top / count_y) - speed_top
    speed_z = (across_z.astype(jnp.float32) + 0.5) * (2.0 * speed_top / count_z) - speed_top
    return speed_x, speed_y, speed_z


def wall_shape(wall_temp, speed_sq):
    temp_cell = wall_temp[..., None]
    return box_volume * jnp.exp(-speed_sq / (2.0 * temp_cell)) / (2.0 * jnp.pi * temp_cell) ** 1.5


def boundary_planes(edge_planes, leaving, entering, wall_profile, inflow, face_type):
    wall_planes = (leaving / entering)[..., None] * wall_profile
    face_kind = face_type[..., None]
    return jnp.where(face_kind == 0, wall_planes, jnp.where(face_kind == 1, inflow, edge_planes))


def transport(current, west_plane, east_plane, speed_x, speed_y, speed_z):
    west_cells = jnp.concatenate([west_plane[None], current[:-1]], 0)
    east_cells = jnp.concatenate([current[1:], east_plane[None]], 0)
    flux_sum = jnp.maximum(speed_x, 0.0) * (current - west_cells) + jnp.minimum(speed_x, 0.0) * (east_cells - current)
    flux_sum = flux_sum + jnp.maximum(speed_y, 0.0) * (current - jnp.roll(current, 1, 1)) + jnp.minimum(speed_y, 0.0) * (jnp.roll(current, -1, 1) - current)
    flux_sum = flux_sum + jnp.maximum(speed_z, 0.0) * (current - jnp.roll(current, 1, 2)) + jnp.minimum(speed_z, 0.0) * (jnp.roll(current, -1, 2) - current)
    return current - courant * flux_sum


def macro_fields(particle_concentration, mean_motion_first_axis, mean_motion_second_axis, mean_motion_third_axis, maxwellian_width, energy_current_first, energy_current_second, energy_current_third):
    kinetic_warmth = maxwellian_width / (3.0 * particle_concentration)
    decay_rate_toward_target = impact_rate_field * particle_concentration * jnp.exp(0.19 * jnp.log(kinetic_warmth))
    return jnp.stack([particle_concentration, mean_motion_first_axis, mean_motion_second_axis, mean_motion_third_axis, kinetic_warmth, energy_current_first, energy_current_second, energy_current_third, decay_rate_toward_target])


def shakhov(params, speed_x, speed_y, speed_z):
    particle_concentration = params[0][..., None]
    peculiar_x = speed_x - params[1][..., None]
    peculiar_y = speed_y - params[2][..., None]
    peculiar_z = speed_z - params[3][..., None]
    temp_cell = params[4][..., None]
    speed_sq = peculiar_x * peculiar_x + peculiar_y * peculiar_y + peculiar_z * peculiar_z
    maxwell = particle_concentration * box_volume * jnp.exp(-speed_sq / (2.0 * temp_cell)) / (2.0 * jnp.pi * temp_cell) ** 1.5
    heat_term = (params[5][..., None] * peculiar_x + params[6][..., None] * peculiar_y + params[7][..., None] * peculiar_z) / (5.0 * particle_concentration * temp_cell * temp_cell)
    return maxwell * (1.0 + shakhov_factor * heat_term * (speed_sq / temp_cell - 5.0))


def relaxation(read, params, speed_x, speed_y, speed_z):
    decay_rate_toward_target = params[8][..., None]
    return (read + decay_rate_toward_target * shakhov(params, speed_x, speed_y, speed_z)) / (1.0 + decay_rate_toward_target)


def central_fields(current, speed_x, speed_y, speed_z, velocity_total):
    particle_concentration = jnp.sum(current, -1) / velocity_total
    mean_motion_first_axis = jnp.sum(current * speed_x, -1) / velocity_total / particle_concentration
    mean_motion_second_axis = jnp.sum(current * speed_y, -1) / velocity_total / particle_concentration
    mean_motion_third_axis = jnp.sum(current * speed_z, -1) / velocity_total / particle_concentration
    peculiar_x = speed_x - mean_motion_first_axis[..., None]
    peculiar_y = speed_y - mean_motion_second_axis[..., None]
    peculiar_z = speed_z - mean_motion_third_axis[..., None]
    speed_sq = peculiar_x * peculiar_x + peculiar_y * peculiar_y + peculiar_z * peculiar_z
    maxwellian_width = jnp.sum(current * speed_sq, -1) / velocity_total
    energy_current_first = 0.5 * jnp.sum(current * peculiar_x * speed_sq, -1) / velocity_total
    energy_current_second = 0.5 * jnp.sum(current * peculiar_y * speed_sq, -1) / velocity_total
    energy_current_third = 0.5 * jnp.sum(current * peculiar_z * speed_sq, -1) / velocity_total
    return macro_fields(particle_concentration, mean_motion_first_axis, mean_motion_second_axis, mean_motion_third_axis, maxwellian_width, energy_current_first, energy_current_second, energy_current_third)


def reference(distribution, inflow, wall_temp, face_type):
    velocity_total = NVX * NVY * NVZ
    speed_x, speed_y, speed_z = velocity_table(NVX, NVY, NVZ, N_VEL)
    speed_sq = speed_x * speed_x + speed_y * speed_y + speed_z * speed_z
    wall_profile = wall_shape(wall_temp, speed_sq)
    outward = jnp.stack([-speed_x, speed_x])[:, None, None, :]
    entering = jnp.sum(wall_profile * jnp.maximum(-outward, 0.0), -1)
    current = distribution
    params = None
    for outer_turn in range(OUTER):
        edge_planes = jnp.stack([current[0], current[-1]])
        leaving = jnp.sum(edge_planes * jnp.maximum(outward, 0.0), -1)
        ghost_planes = boundary_planes(edge_planes, leaving, entering, wall_profile, inflow, face_type)
        read = transport(current, ghost_planes[0], ghost_planes[1], speed_x, speed_y, speed_z)
        current = read
        for inner_turn in range(INNER):
            params = central_fields(current, speed_x, speed_y, speed_z, velocity_total)
            current = relaxation(read, params, speed_x, speed_y, speed_z)
    return current, params[:8]
```

```python
import functools
import math

import jax
import jax.numpy as jnp
import numpy as np
from jax import lax
from jax.experimental import pallas as pl
from jax.experimental.pallas import tpu as pltpu
from jax.sharding import PartitionSpec as P

NVX = 32
NVY = 32
NVZ = 32
OUTER = 2
INNER = 3

BOX = 512.0
TOP = 4.0
COURANT = 0.08
RATE = 0.8
SHAKHOV = 1.0 / 3.0
HIGHEST = lax.Precision.HIGHEST

MOMENTS = [
    [(0, 0, 0)],
    [(1, 0, 0)],
    [(0, 1, 0)],
    [(0, 0, 1)],
    [(2, 0, 0)],
    [(0, 2, 0)],
    [(0, 0, 2)],
    [(1, 1, 0)],
    [(1, 0, 1)],
    [(0, 1, 1)],
    [(3, 0, 0), (1, 2, 0), (1, 0, 2)],
    [(2, 1, 0), (0, 3, 0), (0, 1, 2)],
    [(2, 0, 1), (0, 2, 1), (0, 0, 3)],
]
ROWS = 16
MONOS = 24
SIDES = range(6)


def joined(block, side):
    if any(other // 2 == side // 2 and other != side for other in block):
        return None
    return tuple(sorted(block + (side,)))


BLOCKS1 = [()] + [(side,) for side in SIDES]
BLOCKS2 = list(BLOCKS1)
for _block in BLOCKS1[1:]:
    for _side in SIDES:
        _both = joined(_block, _side)
        if _both is not None and _both not in BLOCKS2:
            BLOCKS2.append(_both)
PLACE = {block: index for index, block in enumerate(BLOCKS2)}
X_BLOCKS = [
    [(first, PLACE[joined(block, side)]) for first, block in enumerate(BLOCKS1) if joined(block, side)]
    for side in (0, 1)
]


def levels(count):
    return (np.arange(count) + 0.5) * (2.0 * TOP / count) - TOP


def factor(values, power, sides):
    result = values**power
    for side in sides:
        result = result * np.maximum(values if side % 2 == 0 else -values, 0.0)
    return result


def axis_sides(block, axis):
    return tuple(side for side in block if side // 2 == axis)


@functools.cache
def tables():
    speeds = [levels(NVX), levels(NVY), levels(NVZ)]
    pairs = {}
    entries = []
    for index, block in enumerate(BLOCKS2):
        for row, monos in enumerate(MOMENTS):
            for mono in monos:
                key = (mono[1], axis_sides(block, 1), mono[2], axis_sides(block, 2))
                place = pairs.setdefault(key, len(pairs))
                entries.append((index * ROWS + row, place, mono[0], axis_sides(block, 0)))
    count = -(-len(pairs) // 8) * 8
    across = np.zeros((count, NVY * NVZ), np.float32)
    for (power_y, sides_y, power_z, sides_z), place in pairs.items():
        product = factor(speeds[1], power_y, sides_y)[:, None] * factor(speeds[2], power_z, sides_z)[None]
        across[place] = product.reshape(-1)
    along = np.zeros((NVX, len(BLOCKS2) * ROWS, count), np.float32)
    for row, place, power, sides in entries:
        along[:, row, place] += factor(speeds[0], power, sides)
    single = np.zeros((3, len(BLOCKS1) * MONOS, NVX), np.float32)
    collect = np.zeros((ROWS, MONOS), np.float32)
    for index, block in enumerate(BLOCKS1):
        mono_row = 0
        for row, monos in enumerate(MOMENTS):
            for mono in monos:
                for axis in range(3):
                    single[axis, index * MONOS + mono_row] = factor(
                        speeds[axis], mono[axis], axis_sides(block, axis)
                    )
                collect[row, mono_row] = 1.0
                mono_row += 1
    return across, along, single, collect


def shift(value, places):
    size = value.shape[-1]
    return pltpu.roll(value, places % size, value.ndim - 1)


def upwind(value, side, depth):
    step = 1 if side % 2 == 0 else -1
    if side // 2 == 1:
        return shift(value, step * depth)
    cell = lax.broadcasted_iota(jnp.int32, value.shape, value.ndim - 1) % depth
    edge = cell == (0 if step == 1 else depth - 1)
    return jnp.where(edge, shift(value, step - step * depth), shift(value, step))


def macro(moments):
    m = [moments[row : row + 1] * (1.0 / (NVX * NVY * NVZ)) for row in range(13)]
    density = m[0]
    u = [m[1] / density, m[2] / density, m[3] / density]
    energy = m[4] + m[5] + m[6]
    u_sq = u[0] * u[0] + u[1] * u[1] + u[2] * u[2]
    temp = (energy - density * u_sq) / (3.0 * density)
    second = [[m[4], m[7], m[8]], [m[7], m[5], m[9]], [m[8], m[9], m[6]]]
    q = []
    for a in range(3):
        cross = u[0] * second[a][0] + u[1] * second[a][1] + u[2] * second[a][2]
        q.append(0.5 * (m[10 + a] - 2.0 * cross - u[a] * energy + 2.0 * density * u_sq * u[a]))
    rate = RATE * density * jnp.exp(0.19 * jnp.log(temp))
    return density, u, temp, q, rate


def equilibrium_moments(density, u, temp, q, single, collect, blocks):
    rows = blocks * MONOS
    sums = []
    for axis in range(3):
        count = (NVX, NVY, NVZ)[axis]
        cells = density.shape[-1]
        level = lax.broadcasted_iota(jnp.int32, (count, cells), 0).astype(jnp.float32)
        offset = (level + 0.5) * (2.0 * TOP / count) - TOP - u[axis]
        weight = jnp.exp(-offset * offset / (2.0 * temp))
        powers = []
        for power in range(4 if q is not None else 1):
            powers.append(
                jnp.dot(
                    single[axis, :rows], weight, precision=HIGHEST, preferred_element_type=jnp.float32
                )
            )
            weight = weight * offset
        sums.append(powers)
    total = sums[0][0] * sums[1][0] * sums[2][0]
    if q is not None:
        tail = SHAKHOV / (5.0 * density * temp * temp)
        inverse = 1.0 / temp
        extra = 0.0
        for a in range(3):
            b, c = (a + 1) % 3, (a + 2) % 3
            fa, fb, fc = sums[a], sums[b], sums[c]
            term = (fa[3] * inverse - 5.0 * fa[1]) * (fb[0] * fc[0])
            term = term + fa[1] * inverse * (fb[2] * fc[0] + fb[0] * fc[2])
            extra = extra + (q[a] * tail) * term
        total = total + extra
    turn = 2.0 * math.pi * temp
    total = total * (density * BOX / (turn * jnp.sqrt(turn)))
    return [
        jnp.dot(
            collect[...],
            total[index * MONOS : (index + 1) * MONOS],
            precision=HIGHEST,
            preferred_element_type=jnp.float32,
        )
        for index in range(blocks)
    ]


def iterate(moments, single, collect):
    current = moments
    for turn in range(INNER):
        fields = macro(current)
        if turn < INNER - 1:
            (target,) = equilibrium_moments(*fields[:4], single, collect, 1)
            current = (moments + fields[4] * target) / (1.0 + fields[4])
    return fields


def ghost_block(wall, inflow, edge, kind):
    return jnp.where(kind == 0, wall, jnp.where(kind == 1, inflow, edge))


def stack_fields(fields):
    density, u, temp, q, rate = fields
    rows = [density, *u, temp, *q, rate]
    return jnp.concatenate(rows + [jnp.zeros_like(density)] * (ROWS - len(rows)), 0)


def chain1_kernel(axis_name, depth, sums, west, east, inflow, wall_temp, kind, single, single_x, collect,
                  fields_out, flux_out, first_out):
    place = lax.axis_index(axis_name)
    ends = (place == 0, place == lax.axis_size(axis_name) - 1)
    got = (west, east)
    kinds = [kind[face : face + 1] for face in range(2)]
    walls, entering, ratios = [], [], []
    for face in range(2):
        temp = wall_temp[face : face + 1]
        one = jnp.ones_like(temp)
        zero = jnp.zeros_like(temp)
        wall = equilibrium_moments(one, [zero] * 3, temp, None, single_x.at[face], collect, 6)
        walls.append(wall)
        entering.append(wall[0][0:1])
        ratios.append(sums[2 - face][0:1] / wall[0][0:1])
    read = []
    for first, block in enumerate(BLOCKS1):
        value = sums[first]
        flux = jnp.zeros_like(value)
        for side in SIDES:
            both = joined(block, side)
            if both is None:
                continue
            own = sums[PLACE[both]]
            if side < 2:
                slot = [entry[0] for entry in X_BLOCKS[side]].index(first)
                ghost = ghost_block(ratios[side] * walls[side][slot], inflow[side, slot], own, kinds[side])
                other = jnp.where(ends[side], ghost, got[side][slot])
            else:
                other = upwind(own, side, depth)
            flux = flux + (own - other)
        read.append(value - COURANT * flux)
    fields = iterate(read[0], single, collect)
    target = equilibrium_moments(*fields[:4], single, collect, len(BLOCKS1))
    rate = fields[4]
    after = [(value + rate * goal) / (1.0 + rate) for value, goal in zip(read, target)]
    stacked = stack_fields(fields)
    scale = []
    for face in range(2):
        temp = wall_temp[face : face + 1]
        turn = 2.0 * math.pi * temp
        norm = BOX / (turn * jnp.sqrt(turn))
        ratio2 = after[2 - face][0:1] / entering[face]
        scale.append((ratios[face] * norm, ratio2 * norm, ratio2))
    fields_out[...] = jnp.concatenate(
        [stacked[:9], scale[0][0], scale[0][1], scale[1][0], scale[1][1], stacked[13:]], 0
    )
    for index in range(len(BLOCKS1)):
        flux_out[index] = after[index]
    for face in range(2):
        first_out[face] = ghost_block(
            scale[face][2] * walls[face][0], inflow[face, 0], after[1 + face], kinds[face]
        )


def chain2_kernel(axis_name, depth, after, west, east, ghosts, single, collect, fields_out):
    place = lax.axis_index(axis_name)
    ends = (place == 0, place == lax.axis_size(axis_name) - 1)
    got = (west, east)
    flux = jnp.zeros_like(after[0])
    for side in SIDES:
        own = after[1 + side]
        if side < 2:
            other = jnp.where(ends[side], ghosts[side], got[side][...])
        else:
            other = upwind(own, side, depth)
        flux = flux + (own - other)
    fields = iterate(after[0] - COURANT * flux, single, collect)
    fields_out[...] = stack_fields(fields)


def step_tile(center, up, speeds, params, base):
    cx, cy, cz = speeds
    ax, ay, az = jnp.abs(cx), jnp.abs(cy), jnp.abs(cz)
    rows, depth = center.shape[:2]
    up_y = jnp.where(
        cy > 0.0,
        jnp.concatenate([center[rows - 1 :], center[: rows - 1]], 0),
        jnp.concatenate([center[1:], center[:1]], 0),
    )
    up_z = jnp.where(cz > 0.0, pltpu.roll(center, 1, 1), pltpu.roll(center, depth - 1, 1))
    read = center * (1.0 - COURANT * (ax + ay + az)) + COURANT * (ax * up + ay * up_y + az * up_z)
    column = lambda k: params[:, :, base + k : base + k + 1]
    px, py, pz = cx - column(0), cy - column(1), cz - column(2)
    inverse = column(3)
    r = (px * px + py * py + pz * pz) * inverse
    heat = column(4) * px + column(5) * py + column(6) * pz
    goal = column(7) * jnp.exp(-0.5 * r) * (1.0 + heat * (r - 5.0))
    return read * column(8) + goal


def cell_kernel(axis_name, half_blocks, own, west1, east1, west2, east2, inflow, speeds, params, out, mid, side_mid):
    place = lax.axis_index(axis_name)
    last = lax.axis_size(axis_name) - 1
    block = pl.program_id(0)

    def half(face, up1, up2):
        distance = place if face == 0 else last - place
        par = params.at[face]

        def ghost(edge, c, scale_column, lanes):
            c_sq = c[0] * c[0] + c[1] * c[1] + c[2] * c[2]
            kind = par[:, :, 27:28]
            wall = par[:, :, scale_column : scale_column + 1] * jnp.exp(-c_sq * par[:, :, 28:29])
            return jnp.where(kind == 0.0, wall, jnp.where(kind == 1.0, inflow[0, :, :, lanes], edge))

        def tile(index, carry):
            lanes = pl.ds(pl.multiple_of(index * 128, 128), 128)
            c = tuple(speeds[k : k + 1, lanes] for k in range(3))

            @pl.when(distance == 0)
            def _():
                center = own[0, :, :, lanes]
                value = step_tile(center, ghost(center, c, 29, lanes), c, par, 0)
                mid[...] = value
                side_mid[...] = ghost(value, c, 30, lanes)

            @pl.when(distance > 0)
            def _():
                mid[...] = step_tile(own[0, :, :, lanes], up1[:, :, lanes], c, par, 0)

            @pl.when(distance == 1)
            def _():
                center = up1[:, :, lanes]
                side_mid[...] = step_tile(center, ghost(center, c, 29, lanes), c, par, 9)

            @pl.when(distance > 1)
            def _():
                side_mid[...] = step_tile(up1[:, :, lanes], up2[:, :, lanes], c, par, 9)

            out[0, :, :, lanes] = step_tile(mid[...], side_mid[...], c, par, 18)
            return carry

        lax.fori_loop(0, out.shape[3] // 128, tile, 0)

    @pl.when(block < half_blocks)
    def _():
        half(1, east1, east2)

    @pl.when(block >= half_blocks)
    def _():
        half(0, west1, west2)


def passed_along(value, axis, steps):
    count = lax.axis_size(axis)
    leading, last = (max(0, -steps), min(count, count - steps))
    return lax.ppermute(value, axis, [(source, source + steps) for source in range(leading, last)])


def relax_columns(fields):
    density, temp, rate = fields[0], fields[4], fields[8]
    turn = 2.0 * math.pi * temp
    keep = 1.0 / (1.0 + rate)
    tail = SHAKHOV / (5.0 * density * temp * temp)
    return [
        fields[1],
        fields[2],
        fields[3],
        1.0 / temp,
        fields[5] * tail,
        fields[6] * tail,
        fields[7] * tail,
        density * BOX / (turn * jnp.sqrt(turn)) * rate * keep,
        keep,
    ]


def body(distribution, inflow, wall_temp, face_type):
    slabs, rows, depth, local = distribution.shape
    cells = rows * depth
    halves = local // 2
    layer = NVY * NVZ
    group = min(halves, layer)
    vel = lax.axis_index("vel")
    across, along, single, collect = tables()

    positive = distribution[0, :, :, halves:]
    negative = distribution[0, :, :, :halves]
    west1 = passed_along(positive, "space", 1)
    east1 = passed_along(negative, "space", -1)
    west2 = passed_along(positive, "space", 2)
    east2 = passed_along(negative, "space", -2)

    ranked = vel * halves + jnp.arange(local, dtype=jnp.int32) % halves
    sign = jnp.where(jnp.arange(local) < halves, -1.0, 1.0)
    speed_x = sign * ((ranked // layer).astype(jnp.float32) + 0.5) * (2.0 * TOP / NVX)
    speed_y = (((ranked % layer) // NVZ).astype(jnp.float32) + 0.5) * (2.0 * TOP / NVY) - TOP
    speed_z = ((ranked % NVZ).astype(jnp.float32) + 0.5) * (2.0 * TOP / NVZ) - TOP
    speeds = jnp.stack([speed_x, speed_y, speed_z] + [jnp.zeros_like(speed_x)] * 5)

    def all_moments(parts):
        total = 0.0
        across_all = jnp.asarray(across)
        along_all = jnp.asarray(along)
        for index in range(local // group):
            upper = index * group // halves
            rank = vel * halves + index * group % halves
            level = rank // layer
            level = NVX // 2 + level if upper else NVX // 2 - 1 - level
            table = lax.dynamic_slice_in_dim(across_all, rank % layer, group, 1)
            part = parts[1 if upper else 0][:, index * group % halves : index * group % halves + group]
            inner = lax.dot_general(
                table, part, (((1,), (1,)), ((), ())), precision=HIGHEST,
                preferred_element_type=jnp.float32,
            )
            weight = lax.dynamic_index_in_dim(along_all, level, 0, False)
            total = total + jnp.dot(weight, inner, precision=HIGHEST, preferred_element_type=jnp.float32)
        return total.reshape(len(BLOCKS2), ROWS, cells)

    flat = (negative.reshape(cells, halves), positive.reshape(cells, halves))
    sums = all_moments(flat)
    flat_in = (
        inflow[1, :, :, :halves].reshape(cells, halves),
        inflow[0, :, :, halves:].reshape(cells, halves),
    )
    sums_in = all_moments(flat_in)
    picked = [[place for _, place in X_BLOCKS[side]] for side in (0, 1)]
    inflow_x = jnp.stack([jnp.stack([sums_in[k] for k in picked[side]]) for side in (0, 1)])
    sums, inflow_x = lax.psum((sums, inflow_x), "vel")
    to_east = jnp.stack([sums[k] for k in picked[0]])
    to_west = jnp.stack([sums[k] for k in picked[1]])
    from_west = passed_along(to_east, "space", 1)
    from_east = passed_along(to_west, "space", -1)

    wall_flat = wall_temp.reshape(2, cells)
    kind_flat = face_type.reshape(2, cells)
    spans = [[BLOCKS2[k] for k in picked[side]] for side in (0, 1)]
    speeds_np = [levels(NVX), levels(NVY), levels(NVZ)]
    single_x = np.zeros((2, 3, len(picked[0]) * MONOS, NVX), np.float32)
    for side in (0, 1):
        for index, block in enumerate(spans[side]):
            mono_row = 0
            for monos in MOMENTS:
                for mono in monos:
                    for axis in range(3):
                        single_x[side, axis, index * MONOS + mono_row] = factor(
                            speeds_np[axis], mono[axis], axis_sides(block, axis)
                        )
                    mono_row += 1

    shape = functools.partial(jax.ShapeDtypeStruct, dtype=jnp.float32)
    big = pltpu.CompilerParams(vmem_limit_bytes=48 * 1024 * 1024)
    fields1, after, ghosts = pl.pallas_call(
        functools.partial(chain1_kernel, "space", depth),
        out_shape=(
            shape((ROWS, cells)),
            shape((len(BLOCKS1), ROWS, cells)),
            shape((2, ROWS, cells)),
        ),
        compiler_params=big,
        name="first_moments",
    )(
        sums, from_west, from_east, inflow_x, wall_flat, kind_flat,
        jnp.asarray(single), jnp.asarray(single_x), jnp.asarray(collect),
    )
    west_in = passed_along(jnp.concatenate([fields1, after[1]], 0), "space", 1)
    east_in = passed_along(jnp.concatenate([fields1, after[2]], 0), "space", -1)
    fields2 = pl.pallas_call(
        functools.partial(chain2_kernel, "space", depth),
        out_shape=shape((ROWS, cells)),
        compiler_params=big,
        name="second_moments",
    )(after, west_in[ROWS:], east_in[ROWS:], ghosts, jnp.asarray(single), jnp.asarray(collect))

    place = lax.axis_index("space")
    last = lax.axis_size("space") - 1
    half_params = []
    own_columns = relax_columns(fields1)
    last_columns = relax_columns(fields2)
    for face, near in ((0, west_in), (1, east_in)):
        at_end = place == (0 if face == 0 else last)
        first_scale = jnp.where(at_end, fields1[9 + 2 * face], near[9 + 2 * face])
        columns = own_columns + relax_columns(near) + last_columns
        columns += [
            kind_flat[face].astype(jnp.float32),
            0.5 / wall_flat[face],
            first_scale,
            fields1[10 + 2 * face],
        ]
        columns += [jnp.zeros_like(first_scale)] * (32 - len(columns))
        half_params.append(jnp.stack(columns, -1).reshape(rows, depth, 32))
    params = jnp.stack(half_params)

    width = min(512, halves)
    half_blocks = halves // width
    low = lambda i: (0, 0, jnp.minimum(i, half_blocks - 1))
    high = lambda i: (0, 0, jnp.maximum(i - half_blocks, 0))
    plane = (rows, depth, width)
    updated = pl.pallas_call(
        functools.partial(cell_kernel, "space", half_blocks),
        grid=(2 * half_blocks,),
        in_specs=[
            pl.BlockSpec((1,) + plane, lambda i: (0, 0, 0, i)),
            pl.BlockSpec(plane, high),
            pl.BlockSpec(plane, low),
            pl.BlockSpec(plane, high),
            pl.BlockSpec(plane, low),
            pl.BlockSpec((1,) + plane, lambda i: (jnp.where(i < half_blocks, 1, 0), 0, 0, i)),
            pl.BlockSpec((8, width), lambda i: (0, i)),
            pl.BlockSpec((2, rows, depth, 32), lambda i: (0, 0, 0, 0)),
        ],
        out_specs=pl.BlockSpec((1,) + plane, lambda i: (0, 0, 0, i)),
        out_shape=shape(distribution.shape),
        scratch_shapes=[pltpu.VMEM((rows, depth, 128), jnp.float32)] * 2,
        compiler_params=big,
        name="two_steps",
    )(distribution, west1, east1, west2, east2, inflow, speeds, params)
    fields = fields2[:8].reshape(8, 1, rows, depth)
    return updated, fields


def solution(mesh):
    in_specs = (P("space", None, None, "vel"), P(None, None, None, "vel"), P(), P())
    out_specs = (P("space", None, None, "vel"), P(None, "space", None, None))
    return jax.shard_map(body, mesh=mesh, in_specs=in_specs, out_specs=out_specs, check_vma=False)
```

```python
import functools
import math

import jax
import jax.numpy as jnp
import numpy as np
from jax import lax
from jax.experimental import pallas as pl
from jax.experimental.pallas import tpu as pltpu
from jax.sharding import PartitionSpec as P

NVX = 32
NVY = 32
NVZ = 32
OUTER = 2
INNER = 3

BOX = 512.0
TOP = 4.0
COURANT = 0.08
RATE = 0.8
SHAKHOV = 1.0 / 3.0
HIGHEST = lax.Precision.HIGHEST

MOMENTS = [
    [(0, 0, 0)],
    [(1, 0, 0)],
    [(0, 1, 0)],
    [(0, 0, 1)],
    [(2, 0, 0)],
    [(0, 2, 0)],
    [(0, 0, 2)],
    [(1, 1, 0)],
    [(1, 0, 1)],
    [(0, 1, 1)],
    [(3, 0, 0), (1, 2, 0), (1, 0, 2)],
    [(2, 1, 0), (0, 3, 0), (0, 1, 2)],
    [(2, 0, 1), (0, 2, 1), (0, 0, 3)],
]
ROWS = 16
COLUMNS = 32
MONOS = 24
SIDES = range(6)


def joined(block, side):
    if any(other // 2 == side // 2 and other != side for other in block):
        return None
    return tuple(sorted(block + (side,)))


BLOCKS1 = [()] + [(side,) for side in SIDES]
BLOCKS2 = list(BLOCKS1)
for _block in BLOCKS1[1:]:
    for _side in SIDES:
        _both = joined(_block, _side)
        if _both is not None and _both not in BLOCKS2:
            BLOCKS2.append(_both)
PLACE = {block: index for index, block in enumerate(BLOCKS2)}
X_BLOCKS = [
    [(first, PLACE[joined(block, side)]) for first, block in enumerate(BLOCKS1) if joined(block, side)]
    for side in (0, 1)
]


def levels(count):
    return (np.arange(count) + 0.5) * (2.0 * TOP / count) - TOP


def factor(values, power, sides):
    result = values**power
    for side in sides:
        result = result * np.maximum(values if side % 2 == 0 else -values, 0.0)
    return result


def axis_sides(block, axis):
    return tuple(side for side in block if side // 2 == axis)


@functools.cache
def tables():
    speeds = [levels(NVX), levels(NVY), levels(NVZ)]
    pairs = {}
    entries = []
    for index, block in enumerate(BLOCKS2):
        for row, monos in enumerate(MOMENTS):
            for mono in monos:
                key = (mono[1], axis_sides(block, 1), mono[2], axis_sides(block, 2))
                place = pairs.setdefault(key, len(pairs))
                entries.append((index * ROWS + row, place, mono[0], axis_sides(block, 0)))
    count = -(-len(pairs) // 8) * 8
    across = np.zeros((count, NVY * NVZ), np.float32)
    for (power_y, sides_y, power_z, sides_z), place in pairs.items():
        product = factor(speeds[1], power_y, sides_y)[:, None] * factor(speeds[2], power_z, sides_z)[None]
        across[place] = product.reshape(-1)
    along = np.zeros((NVX, len(BLOCKS2) * ROWS, count), np.float32)
    for row, place, power, sides in entries:
        along[:, row, place] += factor(speeds[0], power, sides)
    along_x = np.zeros((NVX, len(X_BLOCKS[0]) * ROWS, count), np.float32)
    for level in range(NVX):
        side = 0 if level >= NVX // 2 else 1
        for slot, (_, index) in enumerate(X_BLOCKS[side]):
            along_x[level, slot * ROWS : (slot + 1) * ROWS] = along[level, index * ROWS : (index + 1) * ROWS]
    single = np.zeros((3, len(BLOCKS1) * MONOS, NVX), np.float32)
    collect = np.zeros((ROWS, MONOS), np.float32)
    for index, block in enumerate(BLOCKS1):
        mono_row = 0
        for row, monos in enumerate(MOMENTS):
            for mono in monos:
                for axis in range(3):
                    single[axis, index * MONOS + mono_row] = factor(
                        speeds[axis], mono[axis], axis_sides(block, axis)
                    )
                collect[row, mono_row] = 1.0
                mono_row += 1
    return across, along, along_x, single, collect


def shift(value, places):
    size = value.shape[-1]
    return pltpu.roll(value, places % size, value.ndim - 1)


def upwind(value, side, depth):
    step = 1 if side % 2 == 0 else -1
    if side // 2 == 1:
        return shift(value, step * depth)
    cell = lax.broadcasted_iota(jnp.int32, value.shape, value.ndim - 1) % depth
    edge = cell == (0 if step == 1 else depth - 1)
    return jnp.where(edge, shift(value, step - step * depth), shift(value, step))


def macro(moments):
    m = [moments[row : row + 1] * (1.0 / (NVX * NVY * NVZ)) for row in range(13)]
    density = m[0]
    u = [m[1] / density, m[2] / density, m[3] / density]
    energy = m[4] + m[5] + m[6]
    u_sq = u[0] * u[0] + u[1] * u[1] + u[2] * u[2]
    temp = (energy - density * u_sq) / (3.0 * density)
    second = [[m[4], m[7], m[8]], [m[7], m[5], m[9]], [m[8], m[9], m[6]]]
    q = []
    for a in range(3):
        cross = u[0] * second[a][0] + u[1] * second[a][1] + u[2] * second[a][2]
        q.append(0.5 * (m[10 + a] - 2.0 * cross - u[a] * energy + 2.0 * density * u_sq * u[a]))
    rate = RATE * density * jnp.exp(0.19 * jnp.log(temp))
    return density, u, temp, q, rate


def equilibrium_moments(density, u, temp, q, single, collect, blocks):
    rows = blocks * MONOS
    sums = []
    for axis in range(3):
        count = (NVX, NVY, NVZ)[axis]
        cells = density.shape[-1]
        level = lax.broadcasted_iota(jnp.int32, (count, cells), 0).astype(jnp.float32)
        offset = (level + 0.5) * (2.0 * TOP / count) - TOP - u[axis]
        weight = jnp.exp(-offset * offset / (2.0 * temp))
        powers = []
        for power in range(4 if q is not None else 1):
            powers.append(
                jnp.dot(
                    single[axis, :rows], weight, precision=HIGHEST, preferred_element_type=jnp.float32
                )
            )
            weight = weight * offset
        sums.append(powers)
    total = sums[0][0] * sums[1][0] * sums[2][0]
    if q is not None:
        tail = SHAKHOV / (5.0 * density * temp * temp)
        inverse = 1.0 / temp
        extra = 0.0
        for a in range(3):
            b, c = (a + 1) % 3, (a + 2) % 3
            fa, fb, fc = sums[a], sums[b], sums[c]
            term = (fa[3] * inverse - 5.0 * fa[1]) * (fb[0] * fc[0])
            term = term + fa[1] * inverse * (fb[2] * fc[0] + fb[0] * fc[2])
            extra = extra + (q[a] * tail) * term
        total = total + extra
    turn = 2.0 * math.pi * temp
    total = total * (density * BOX / (turn * jnp.sqrt(turn)))
    return [
        jnp.dot(
            collect[...],
            total[index * MONOS : (index + 1) * MONOS],
            precision=HIGHEST,
            preferred_element_type=jnp.float32,
        )
        for index in range(blocks)
    ]


def iterate(moments, single, collect):
    current = moments
    for turn in range(INNER):
        fields = macro(current)
        if turn < INNER - 1:
            (target,) = equilibrium_moments(*fields[:4], single, collect, 1)
            current = (moments + fields[4] * target) / (1.0 + fields[4])
    return fields


def ghost_block(wall, inflow, edge, kind):
    return jnp.where(kind == 0, wall, jnp.where(kind == 1, inflow, edge))


def stack_fields(fields):
    density, u, temp, q, rate = fields
    rows = [density, *u, temp, *q, rate]
    return jnp.concatenate(rows + [jnp.zeros_like(density)] * (ROWS - len(rows)), 0)


def chain1_kernel(axis_name, depth, sums, west, east, inflow, wall_temp, kind, single, single_x, collect,
                  west_out, east_out, flux_out, first_out):
    place = lax.axis_index(axis_name)
    ends = (place == 0, place == lax.axis_size(axis_name) - 1)
    got = (west, east)
    kinds = [kind[face : face + 1] for face in range(2)]
    walls, entering, ratios = [], [], []
    for face in range(2):
        temp = wall_temp[face : face + 1]
        one = jnp.ones_like(temp)
        zero = jnp.zeros_like(temp)
        wall = equilibrium_moments(one, [zero] * 3, temp, None, single_x.at[face], collect, 6)
        walls.append(wall)
        entering.append(wall[0][0:1])
        ratios.append(sums[2 - face][0:1] / wall[0][0:1])
    read = []
    for first, block in enumerate(BLOCKS1):
        value = sums[first]
        flux = jnp.zeros_like(value)
        for side in SIDES:
            both = joined(block, side)
            if both is None:
                continue
            own = sums[PLACE[both]]
            if side < 2:
                slot = [entry[0] for entry in X_BLOCKS[side]].index(first)
                ghost = ghost_block(ratios[side] * walls[side][slot], inflow[slot], own, kinds[side])
                other = jnp.where(ends[side], ghost, got[side][slot])
            else:
                other = upwind(own, side, depth)
            flux = flux + (own - other)
        read.append(value - COURANT * flux)
    fields = iterate(read[0], single, collect)
    target = equilibrium_moments(*fields[:4], single, collect, len(BLOCKS1))
    rate = fields[4]
    after = [(value + rate * goal) / (1.0 + rate) for value, goal in zip(read, target)]
    stacked = stack_fields(fields)
    scale = []
    for face in range(2):
        temp = wall_temp[face : face + 1]
        turn = 2.0 * math.pi * temp
        norm = BOX / (turn * jnp.sqrt(turn))
        ratio2 = after[2 - face][0:1] / entering[face]
        scale.append((ratios[face] * norm, ratio2 * norm, ratio2))
    packed = jnp.concatenate(
        [stacked[:9], scale[0][0], scale[0][1], scale[1][0], scale[1][1], stacked[13:]], 0
    )
    west_out[...] = jnp.concatenate([packed, after[1]], 0)
    east_out[...] = jnp.concatenate([packed, after[2]], 0)
    for index in range(len(BLOCKS1)):
        flux_out[index] = after[index]
    for face in range(2):
        first_out[face] = ghost_block(
            scale[face][2] * walls[face][0], inflow[0], after[1 + face], kinds[face]
        )


def relax_rows(fields):
    row = lambda k: fields[k : k + 1]
    density, temp, rate = row(0), row(4), row(8)
    turn = 2.0 * math.pi * temp
    keep = 1.0 / (1.0 + rate)
    tail = SHAKHOV / (5.0 * density * temp * temp)
    return [
        row(1),
        row(2),
        row(3),
        1.0 / temp,
        row(5) * tail,
        row(6) * tail,
        row(7) * tail,
        density * BOX / (turn * jnp.sqrt(turn)) * rate * keep,
        keep,
    ]


def chain2_kernel(axis_name, depth, own_pack, after, west, east, ghosts, wall_temp, kind, single, collect,
                  fields_out, params_out):
    place = lax.axis_index(axis_name)
    ends = (place == 0, place == lax.axis_size(axis_name) - 1)
    got = (west, east)
    flux = jnp.zeros_like(after[0])
    for side in SIDES:
        own = after[1 + side]
        if side < 2:
            other = jnp.where(ends[side], ghosts[side], got[side][ROWS:])
        else:
            other = upwind(own, side, depth)
        flux = flux + (own - other)
    fields = stack_fields(iterate(after[0] - COURANT * flux, single, collect))
    fields_out[...] = fields
    mine = own_pack[:ROWS]
    for face in range(2):
        near = got[face][:ROWS]
        k = 9 + 2 * face
        rows = relax_rows(mine) + relax_rows(near) + relax_rows(fields)
        rows += [
            kind[face : face + 1].astype(jnp.float32),
            0.5 / wall_temp[face : face + 1],
            jnp.where(ends[face], mine[k : k + 1], near[k : k + 1]),
            mine[k + 1 : k + 2],
        ]
        rows += [jnp.zeros_like(rows[0])] * (COLUMNS - len(rows))
        params_out[face] = jnp.concatenate(rows, 0).T


def moment_kernel(half_groups, axis_name, level, own, inflow, across, along, along_x, out, out_x):
    group = pl.program_id(0)
    cells = out.shape[1]

    def sums(ref, weight):
        inner = lax.dot_general(
            across[...], ref[0].reshape(cells, ref.shape[3]), (((1,), (1,)), ((), ())),
            precision=HIGHEST, preferred_element_type=jnp.float32,
        )
        return jnp.dot(weight[0], inner, precision=HIGHEST, preferred_element_type=jnp.float32)

    @pl.when(group == 0)
    def _():
        out[...] = jnp.zeros_like(out)
        out_x[...] = jnp.zeros_like(out_x)

    out[...] += sums(own, along)

    @pl.when((group >= half_groups) == (lax.axis_index(axis_name) == 0))
    def _():
        out_x[...] += sums(inflow, along_x)


def transported(center, up, c):
    cx, cy, cz = c
    ax, ay, az = COURANT * jnp.abs(cx), COURANT * jnp.abs(cy), COURANT * jnp.abs(cz)
    rows, depth = center.shape[:2]
    up_y = jnp.where(
        cy > 0.0,
        jnp.concatenate([center[rows - 1 :], center[: rows - 1]], 0),
        jnp.concatenate([center[1:], center[:1]], 0),
    )
    up_z = jnp.where(cz > 0.0, pltpu.roll(center, 1, 1), pltpu.roll(center, depth - 1, 1))
    return center * (1.0 - (ax + ay + az)) + (ax * up + ay * up_y + az * up_z)


def cell_kernel(axis_name, half_blocks, own, west1, east1, west2, east2, inflow, speeds, params, out,
                wide, part_r, part_h, mid, side_mid):
    place = lax.axis_index(axis_name)
    last = lax.axis_size(axis_name) - 1
    block = pl.program_id(0)

    @pl.when(block % half_blocks == 0)
    def _():
        face = jnp.where(block < half_blocks, 1, 0)
        for k in range(31):
            wide[k] = jnp.broadcast_to(params[face, :, :, k : k + 1], wide.shape[1:])

    for turn in range(3):
        base = 9 * turn
        px = speeds[0:1, :128] - wide[base]
        pz = speeds[2:3, :128] - wide[base + 2]
        part_r[turn] = (px * px + pz * pz) * wide[base + 3]
        part_h[turn] = wide[base + 4] * px + wide[base + 6] * pz

    def step(center, up, c, turn):
        base = 9 * turn
        read = transported(center, up, c)
        py = c[1] - wide[base + 1]
        r = part_r[turn] + py * py * wide[base + 3]
        heat = part_h[turn] + py * wide[base + 5]
        goal = wide[base + 7] * jnp.exp(-0.5 * r) * (1.0 + heat * (r - 5.0))
        return read * wide[base + 8] + goal

    def half(face, up1, up2):
        distance = place if face == 0 else last - place

        def ghost(edge, c, scale_column, lanes):
            c_sq = c[0] * c[0] + c[1] * c[1] + c[2] * c[2]
            kind = wide[27]
            wall = wide[scale_column] * jnp.exp(-c_sq * wide[28])
            return jnp.where(kind == 0.0, wall, jnp.where(kind == 1.0, inflow[0, :, :, lanes], edge))

        def tile(index, carry):
            lanes = pl.ds(pl.multiple_of(index * 128, 128), 128)
            c = tuple(speeds[k : k + 1, lanes] for k in range(3))

            @pl.when(distance == 0)
            def _():
                center = own[0, :, :, lanes]
                value = step(center, ghost(center, c, 29, lanes), c, 0)
                mid[...] = value
                side_mid[...] = ghost(value, c, 30, lanes)

            @pl.when(distance > 0)
            def _():
                mid[...] = step(own[0, :, :, lanes], up1[:, :, lanes], c, 0)

            @pl.when(distance == 1)
            def _():
                center = up1[:, :, lanes]
                side_mid[...] = step(center, ghost(center, c, 29, lanes), c, 1)

            @pl.when(distance > 1)
            def _():
                side_mid[...] = step(up1[:, :, lanes], up2[:, :, lanes], c, 1)

            out[0, :, :, lanes] = step(mid[...], side_mid[...], c, 2)
            return carry

        lax.fori_loop(0, out.shape[3] // 128, tile, 0)

    @pl.when(block < half_blocks)
    def _():
        half(1, east1, east2)

    @pl.when(block >= half_blocks)
    def _():
        half(0, west1, west2)


def passed_along(value, axis, steps):
    count = lax.axis_size(axis)
    leading, last = (max(0, -steps), min(count, count - steps))
    return lax.ppermute(value, axis, [(source, source + steps) for source in range(leading, last)])


def body(distribution, inflow, wall_temp, face_type):
    slabs, rows, depth, local = distribution.shape
    cells = rows * depth
    halves = local // 2
    layer = NVY * NVZ
    group = min(halves, layer)
    vel = lax.axis_index("vel")
    across, along, along_x, single, collect = tables()

    positive = distribution[0, :, :, halves:]
    negative = distribution[0, :, :, :halves]
    west1 = passed_along(positive, "space", 1)
    east1 = passed_along(negative, "space", -1)
    west2 = passed_along(positive, "space", 2)
    east2 = passed_along(negative, "space", -2)

    ranked = vel * halves + jnp.arange(local, dtype=jnp.int32) % halves
    sign = jnp.where(jnp.arange(local) < halves, -1.0, 1.0)
    speed_x = sign * ((ranked // layer).astype(jnp.float32) + 0.5) * (2.0 * TOP / NVX)
    speed_y = (((ranked % layer) // NVZ).astype(jnp.float32) + 0.5) * (2.0 * TOP / NVY) - TOP
    speed_z = ((ranked % NVZ).astype(jnp.float32) + 0.5) * (2.0 * TOP / NVZ) - TOP
    speeds = jnp.stack([speed_x, speed_y, speed_z] + [jnp.zeros_like(speed_x)] * 5)

    shape = functools.partial(jax.ShapeDtypeStruct, dtype=jnp.float32)
    big = pltpu.CompilerParams(vmem_limit_bytes=48 * 1024 * 1024)
    picked = [[index for _, index in X_BLOCKS[side]] for side in (0, 1)]
    half_groups = halves // group
    level = (vel * halves + jnp.arange(half_groups, dtype=jnp.int32) * group) // layer
    level = jnp.concatenate([NVX // 2 - 1 - level, NVX // 2 + level])
    table = lax.dynamic_slice_in_dim(jnp.asarray(across), vel * halves % layer, group, 1)
    count = table.shape[0]
    slots = len(picked[0]) * ROWS
    sums, inflow_x = pl.pallas_call(
        functools.partial(moment_kernel, half_groups, "space"),
        grid_spec=pltpu.PrefetchScalarGridSpec(
            num_scalar_prefetch=1,
            grid=(2 * half_groups,),
            in_specs=[
                pl.BlockSpec((1, rows, depth, group), lambda i, lv: (0, 0, 0, i)),
                pl.BlockSpec(
                    (1, rows, depth, group), lambda i, lv: (jnp.where(i < half_groups, 1, 0), 0, 0, i)
                ),
                pl.BlockSpec((count, group), lambda i, lv: (0, 0)),
                pl.BlockSpec((1, len(BLOCKS2) * ROWS, count), lambda i, lv: (lv[i], 0, 0)),
                pl.BlockSpec((1, slots, count), lambda i, lv: (lv[i], 0, 0)),
            ],
            out_specs=[
                pl.BlockSpec((len(BLOCKS2) * ROWS, cells), lambda i, lv: (0, 0)),
                pl.BlockSpec((slots, cells), lambda i, lv: (0, 0)),
            ],
        ),
        out_shape=(shape((len(BLOCKS2) * ROWS, cells)), shape((slots, cells))),
        compiler_params=big,
        name="input_moments",
    )(level, distribution, inflow, table, jnp.asarray(along), jnp.asarray(along_x))
    sums, inflow_x = lax.psum((sums, inflow_x), "vel")
    sums = sums.reshape(len(BLOCKS2), ROWS, cells)
    inflow_x = inflow_x.reshape(len(picked[0]), ROWS, cells)
    to_east = jnp.stack([sums[k] for k in picked[0]])
    to_west = jnp.stack([sums[k] for k in picked[1]])
    from_west = passed_along(to_east, "space", 1)
    from_east = passed_along(to_west, "space", -1)

    wall_flat = wall_temp.reshape(2, cells)
    kind_flat = face_type.reshape(2, cells)
    spans = [[BLOCKS2[k] for k in picked[side]] for side in (0, 1)]
    speeds_np = [levels(NVX), levels(NVY), levels(NVZ)]
    single_x = np.zeros((2, 3, len(picked[0]) * MONOS, NVX), np.float32)
    for side in (0, 1):
        for index, block in enumerate(spans[side]):
            mono_row = 0
            for monos in MOMENTS:
                for mono in monos:
                    for axis in range(3):
                        single_x[side, axis, index * MONOS + mono_row] = factor(
                            speeds_np[axis], mono[axis], axis_sides(block, axis)
                        )
                    mono_row += 1

    west_pack, east_pack, after, ghosts = pl.pallas_call(
        functools.partial(chain1_kernel, "space", depth),
        out_shape=(
            shape((2 * ROWS, cells)),
            shape((2 * ROWS, cells)),
            shape((len(BLOCKS1), ROWS, cells)),
            shape((2, ROWS, cells)),
        ),
        compiler_params=big,
        name="first_moments",
    )(
        sums, from_west, from_east, inflow_x, wall_flat, kind_flat,
        jnp.asarray(single), jnp.asarray(single_x), jnp.asarray(collect),
    )
    west_in = passed_along(west_pack, "space", 1)
    east_in = passed_along(east_pack, "space", -1)
    fields2, params = pl.pallas_call(
        functools.partial(chain2_kernel, "space", depth),
        out_shape=(shape((ROWS, cells)), shape((2, cells, COLUMNS))),
        compiler_params=big,
        name="second_moments",
    )(
        west_pack, after, west_in, east_in, ghosts, wall_flat, kind_flat,
        jnp.asarray(single), jnp.asarray(collect),
    )
    params = params.reshape(2, rows, depth, COLUMNS)

    width = min(512, halves)
    half_blocks = halves // width
    low = lambda i: (0, 0, jnp.minimum(i, half_blocks - 1))
    high = lambda i: (0, 0, jnp.maximum(i - half_blocks, 0))
    plane = (rows, depth, width)
    updated = pl.pallas_call(
        functools.partial(cell_kernel, "space", half_blocks),
        grid=(2 * half_blocks,),
        in_specs=[
            pl.BlockSpec((1,) + plane, lambda i: (0, 0, 0, i)),
            pl.BlockSpec(plane, high),
            pl.BlockSpec(plane, low),
            pl.BlockSpec(plane, high),
            pl.BlockSpec(plane, low),
            pl.BlockSpec((1,) + plane, lambda i: (jnp.where(i < half_blocks, 1, 0), 0, 0, i)),
            pl.BlockSpec((8, width), lambda i: (0, i)),
            pl.BlockSpec((2, rows, depth, COLUMNS), lambda i: (0, 0, 0, 0)),
        ],
        out_specs=pl.BlockSpec((1,) + plane, lambda i: (0, 0, 0, i)),
        out_shape=shape(distribution.shape),
        scratch_shapes=[
            pltpu.VMEM((31, rows, depth, 128), jnp.float32),
            pltpu.VMEM((3, rows, depth, 128), jnp.float32),
            pltpu.VMEM((3, rows, depth, 128), jnp.float32),
            pltpu.VMEM((rows, depth, 128), jnp.float32),
            pltpu.VMEM((rows, depth, 128), jnp.float32),
        ],
        compiler_params=big,
        name="two_steps",
    )(distribution, west1, east1, west2, east2, inflow, speeds, params)
    fields = fields2[:8].reshape(8, 1, rows, depth)
    return updated, fields


def solution(mesh):
    in_specs = (P("space", None, None, "vel"), P(None, None, None, "vel"), P(), P())
    out_specs = (P("space", None, None, "vel"), P(None, "space", None, None))
    return jax.shard_map(body, mesh=mesh, in_specs=in_specs, out_specs=out_specs, check_vma=False)
```

```python
import functools
import math

import jax
import jax.numpy as jnp
import numpy as np
from jax import lax
from jax.experimental import pallas as pl
from jax.experimental.pallas import tpu as pltpu
from jax.sharding import PartitionSpec as P

NVX = 32
NVY = 32
NVZ = 32
OUTER = 2
INNER = 3

BOX = 512.0
TOP = 4.0
COURANT = 0.08
RATE = 0.8
SHAKHOV = 1.0 / 3.0
HIGHEST = lax.Precision.HIGHEST

MOMENTS = [
    [(0, 0, 0)],
    [(1, 0, 0)],
    [(0, 1, 0)],
    [(0, 0, 1)],
    [(2, 0, 0)],
    [(0, 2, 0)],
    [(0, 0, 2)],
    [(1, 1, 0)],
    [(1, 0, 1)],
    [(0, 1, 1)],
    [(3, 0, 0), (1, 2, 0), (1, 0, 2)],
    [(2, 1, 0), (0, 3, 0), (0, 1, 2)],
    [(2, 0, 1), (0, 2, 1), (0, 0, 3)],
]
ROWS = 16
COLUMNS = 32
MONOS = 24
SIDES = range(6)


def joined(block, side):
    if any(other // 2 == side // 2 and other != side for other in block):
        return None
    return tuple(sorted(block + (side,)))


BLOCKS1 = [()] + [(side,) for side in SIDES]
BLOCKS2 = list(BLOCKS1)
for _block in BLOCKS1[1:]:
    for _side in SIDES:
        _both = joined(_block, _side)
        if _both is not None and _both not in BLOCKS2:
            BLOCKS2.append(_both)
PLACE = {block: index for index, block in enumerate(BLOCKS2)}
X_BLOCKS = [
    [(first, PLACE[joined(block, side)]) for first, block in enumerate(BLOCKS1) if joined(block, side)]
    for side in (0, 1)
]


def levels(count):
    return (np.arange(count) + 0.5) * (2.0 * TOP / count) - TOP


def factor(values, power, sides):
    result = values**power
    for side in sides:
        result = result * np.maximum(values if side % 2 == 0 else -values, 0.0)
    return result


def axis_sides(block, axis):
    return tuple(side for side in block if side // 2 == axis)


@functools.cache
def tables():
    speeds = [levels(NVX), levels(NVY), levels(NVZ)]
    pairs = {}
    entries = []
    for index, block in enumerate(BLOCKS2):
        for row, monos in enumerate(MOMENTS):
            for mono in monos:
                key = (mono[1], axis_sides(block, 1), mono[2], axis_sides(block, 2))
                place = pairs.setdefault(key, len(pairs))
                entries.append((index * ROWS + row, place, mono[0], axis_sides(block, 0)))
    count = -(-len(pairs) // 8) * 8
    across = np.zeros((count, NVY * NVZ), np.float32)
    for (power_y, sides_y, power_z, sides_z), place in pairs.items():
        product = factor(speeds[1], power_y, sides_y)[:, None] * factor(speeds[2], power_z, sides_z)[None]
        across[place] = product.reshape(-1)
    along = np.zeros((NVX, len(BLOCKS2) * ROWS, count), np.float32)
    for row, place, power, sides in entries:
        along[:, row, place] += factor(speeds[0], power, sides)
    along_x = np.zeros((NVX, len(X_BLOCKS[0]) * ROWS, count), np.float32)
    for level in range(NVX):
        side = 0 if level >= NVX // 2 else 1
        for slot, (_, index) in enumerate(X_BLOCKS[side]):
            along_x[level, slot * ROWS : (slot + 1) * ROWS] = along[level, index * ROWS : (index + 1) * ROWS]
    single = np.zeros((3, len(BLOCKS1) * MONOS, NVX), np.float32)
    collect = np.zeros((ROWS, MONOS), np.float32)
    for index, block in enumerate(BLOCKS1):
        mono_row = 0
        for row, monos in enumerate(MOMENTS):
            for mono in monos:
                for axis in range(3):
                    single[axis, index * MONOS + mono_row] = factor(
                        speeds[axis], mono[axis], axis_sides(block, axis)
                    )
                collect[row, mono_row] = 1.0
                mono_row += 1
    return across, along, along_x, single, collect


def shift(value, places):
    size = value.shape[-1]
    return pltpu.roll(value, places % size, value.ndim - 1)


def upwind(value, side, depth):
    step = 1 if side % 2 == 0 else -1
    if side // 2 == 1:
        return shift(value, step * depth)
    cell = lax.broadcasted_iota(jnp.int32, value.shape, value.ndim - 1) % depth
    edge = cell == (0 if step == 1 else depth - 1)
    return jnp.where(edge, shift(value, step - step * depth), shift(value, step))


def macro(moments):
    m = [moments[row : row + 1] * (1.0 / (NVX * NVY * NVZ)) for row in range(13)]
    density = m[0]
    u = [m[1] / density, m[2] / density, m[3] / density]
    energy = m[4] + m[5] + m[6]
    u_sq = u[0] * u[0] + u[1] * u[1] + u[2] * u[2]
    temp = (energy - density * u_sq) / (3.0 * density)
    second = [[m[4], m[7], m[8]], [m[7], m[5], m[9]], [m[8], m[9], m[6]]]
    q = []
    for a in range(3):
        cross = u[0] * second[a][0] + u[1] * second[a][1] + u[2] * second[a][2]
        q.append(0.5 * (m[10 + a] - 2.0 * cross - u[a] * energy + 2.0 * density * u_sq * u[a]))
    rate = RATE * density * jnp.exp(0.19 * jnp.log(temp))
    return density, u, temp, q, rate


def equilibrium_moments(density, u, temp, q, single, collect, blocks):
    rows = blocks * MONOS
    sums = []
    for axis in range(3):
        count = (NVX, NVY, NVZ)[axis]
        cells = density.shape[-1]
        level = lax.broadcasted_iota(jnp.int32, (count, cells), 0).astype(jnp.float32)
        offset = (level + 0.5) * (2.0 * TOP / count) - TOP - u[axis]
        weight = jnp.exp(-offset * offset / (2.0 * temp))
        powers = []
        for power in range(4 if q is not None else 1):
            powers.append(
                jnp.dot(
                    single[axis, :rows], weight, precision=HIGHEST, preferred_element_type=jnp.float32
                )
            )
            weight = weight * offset
        sums.append(powers)
    total = sums[0][0] * sums[1][0] * sums[2][0]
    if q is not None:
        tail = SHAKHOV / (5.0 * density * temp * temp)
        inverse = 1.0 / temp
        extra = 0.0
        for a in range(3):
            b, c = (a + 1) % 3, (a + 2) % 3
            fa, fb, fc = sums[a], sums[b], sums[c]
            term = (fa[3] * inverse - 5.0 * fa[1]) * (fb[0] * fc[0])
            term = term + fa[1] * inverse * (fb[2] * fc[0] + fb[0] * fc[2])
            extra = extra + (q[a] * tail) * term
        total = total + extra
    turn = 2.0 * math.pi * temp
    total = total * (density * BOX / (turn * jnp.sqrt(turn)))
    return [
        jnp.dot(
            collect[...],
            total[index * MONOS : (index + 1) * MONOS],
            precision=HIGHEST,
            preferred_element_type=jnp.float32,
        )
        for index in range(blocks)
    ]


def iterate(moments, single, collect):
    current = moments
    for turn in range(INNER):
        fields = macro(current)
        if turn < INNER - 1:
            (target,) = equilibrium_moments(*fields[:4], single, collect, 1)
            current = (moments + fields[4] * target) / (1.0 + fields[4])
    return fields


def ghost_block(wall, inflow, edge, kind):
    return jnp.where(kind == 0, wall, jnp.where(kind == 1, inflow, edge))


def stack_fields(fields):
    density, u, temp, q, rate = fields
    rows = [density, *u, temp, *q, rate]
    return jnp.concatenate(rows + [jnp.zeros_like(density)] * (ROWS - len(rows)), 0)


def chain1_kernel(axis_name, depth, sums, west, east, inflow, wall_temp, kind, single, single_x, collect,
                  west_out, east_out, flux_out, first_out):
    place = lax.axis_index(axis_name)
    ends = (place == 0, place == lax.axis_size(axis_name) - 1)
    got = (west, east)
    kinds = [kind[face : face + 1] for face in range(2)]
    walls, entering, ratios = [], [], []
    for face in range(2):
        temp = wall_temp[face : face + 1]
        one = jnp.ones_like(temp)
        zero = jnp.zeros_like(temp)
        wall = equilibrium_moments(one, [zero] * 3, temp, None, single_x.at[face], collect, 6)
        walls.append(wall)
        entering.append(wall[0][0:1])
        ratios.append(sums[2 - face][0:1] / wall[0][0:1])
    read = []
    for first, block in enumerate(BLOCKS1):
        value = sums[first]
        flux = jnp.zeros_like(value)
        for side in SIDES:
            both = joined(block, side)
            if both is None:
                continue
            own = sums[PLACE[both]]
            if side < 2:
                slot = [entry[0] for entry in X_BLOCKS[side]].index(first)
                ghost = ghost_block(ratios[side] * walls[side][slot], inflow[slot], own, kinds[side])
                other = jnp.where(ends[side], ghost, got[side][slot])
            else:
                other = upwind(own, side, depth)
            flux = flux + (own - other)
        read.append(value - COURANT * flux)
    fields = iterate(read[0], single, collect)
    target = equilibrium_moments(*fields[:4], single, collect, len(BLOCKS1))
    rate = fields[4]
    after = [(value + rate * goal) / (1.0 + rate) for value, goal in zip(read, target)]
    stacked = stack_fields(fields)
    scale = []
    for face in range(2):
        temp = wall_temp[face : face + 1]
        turn = 2.0 * math.pi * temp
        norm = BOX / (turn * jnp.sqrt(turn))
        ratio2 = after[2 - face][0:1] / entering[face]
        scale.append((ratios[face] * norm, ratio2 * norm, ratio2))
    packed = jnp.concatenate(
        [stacked[:9], scale[0][0], scale[0][1], scale[1][0], scale[1][1], stacked[13:]], 0
    )
    west_out[...] = jnp.concatenate([packed, after[1]], 0)
    east_out[...] = jnp.concatenate([packed, after[2]], 0)
    for index in range(len(BLOCKS1)):
        flux_out[index] = after[index]
    for face in range(2):
        first_out[face] = ghost_block(
            scale[face][2] * walls[face][0], inflow[0], after[1 + face], kinds[face]
        )


def relax_rows(fields):
    row = lambda k: fields[k : k + 1]
    density, temp, rate = row(0), row(4), row(8)
    turn = 2.0 * math.pi * temp
    keep = 1.0 / (1.0 + rate)
    tail = SHAKHOV / (5.0 * density * temp * temp)
    return [
        row(1),
        row(2),
        row(3),
        1.0 / temp,
        row(5) * tail,
        row(6) * tail,
        row(7) * tail,
        density * BOX / (turn * jnp.sqrt(turn)) * rate * keep,
        keep,
    ]


def chain2_kernel(axis_name, depth, own_pack, after, west, east, ghosts, wall_temp, kind, single, collect,
                  fields_out, params_out):
    place = lax.axis_index(axis_name)
    ends = (place == 0, place == lax.axis_size(axis_name) - 1)
    got = (west, east)
    flux = jnp.zeros_like(after[0])
    for side in SIDES:
        own = after[1 + side]
        if side < 2:
            other = jnp.where(ends[side], ghosts[side], got[side][ROWS:])
        else:
            other = upwind(own, side, depth)
        flux = flux + (own - other)
    fields = stack_fields(iterate(after[0] - COURANT * flux, single, collect))
    fields_out[...] = fields
    mine = own_pack[:ROWS]
    for face in range(2):
        near = got[face][:ROWS]
        k = 9 + 2 * face
        rows = relax_rows(mine) + relax_rows(near) + relax_rows(fields)
        rows += [
            kind[face : face + 1].astype(jnp.float32),
            0.5 / wall_temp[face : face + 1],
            jnp.where(ends[face], mine[k : k + 1], near[k : k + 1]),
            mine[k + 1 : k + 2],
        ]
        rows += [jnp.zeros_like(rows[0])] * (COLUMNS - len(rows))
        params_out[face] = jnp.concatenate(rows, 0).T


def moment_kernel(half_groups, axis_name, level, own, inflow, across, along, along_x, out, out_x):
    group = pl.program_id(0)
    cells = out.shape[1]

    def sums(ref, weight):
        inner = lax.dot_general(
            across[...], ref[0].reshape(cells, ref.shape[3]), (((1,), (1,)), ((), ())),
            precision=HIGHEST, preferred_element_type=jnp.float32,
        )
        return jnp.dot(weight[0], inner, precision=HIGHEST, preferred_element_type=jnp.float32)

    @pl.when(group == 0)
    def _():
        out[...] = jnp.zeros_like(out)
        out_x[...] = jnp.zeros_like(out_x)

    out[...] += sums(own, along)

    @pl.when((group >= half_groups) == (lax.axis_index(axis_name) == 0))
    def _():
        out_x[...] += sums(inflow, along_x)


def transported(center, up, c):
    cx, cy, cz = c
    ax, ay, az = COURANT * jnp.abs(cx), COURANT * jnp.abs(cy), COURANT * jnp.abs(cz)
    rows, depth = center.shape[:2]
    up_y = jnp.where(
        cy > 0.0,
        jnp.concatenate([center[rows - 1 :], center[: rows - 1]], 0),
        jnp.concatenate([center[1:], center[:1]], 0),
    )
    up_z = jnp.where(cz > 0.0, pltpu.roll(center, 1, 1), pltpu.roll(center, depth - 1, 1))
    return center * (1.0 - (ax + ay + az)) + (ax * up + ay * up_y + az * up_z)


def cell_kernel(axis_name, half_blocks, own, west1, east1, west2, east2, inflow, speeds, params, out,
                wide, part_r, part_h, mid, side_mid):
    place = lax.axis_index(axis_name)
    last = lax.axis_size(axis_name) - 1
    block = pl.program_id(0)

    @pl.when(block % half_blocks == 0)
    def _():
        face = jnp.where(block < half_blocks, 1, 0)
        for k in range(31):
            wide[k] = jnp.broadcast_to(params[face, :, :, k : k + 1], wide.shape[1:])

    for turn in range(3):
        base = 9 * turn
        px = speeds[0:1, :128] - wide[base]
        pz = speeds[2:3, :128] - wide[base + 2]
        part_r[turn] = (px * px + pz * pz) * wide[base + 3]
        part_h[turn] = wide[base + 4] * px + wide[base + 6] * pz

    def step(center, up, c, turn):
        base = 9 * turn
        read = transported(center, up, c)
        py = c[1] - wide[base + 1]
        r = part_r[turn] + py * py * wide[base + 3]
        heat = part_h[turn] + py * wide[base + 5]
        goal = wide[base + 7] * jnp.exp(-0.5 * r) * (1.0 + heat * (r - 5.0))
        return read * wide[base + 8] + goal

    def half(face, up1, up2):
        distance = place if face == 0 else last - place

        def ghost(edge, c, scale_column, lanes):
            c_sq = c[0] * c[0] + c[1] * c[1] + c[2] * c[2]
            kind = wide[27]
            wall = wide[scale_column] * jnp.exp(-c_sq * wide[28])
            return jnp.where(kind == 0.0, wall, jnp.where(kind == 1.0, inflow[0, :, :, lanes], edge))

        def tile(index, carry):
            lanes = pl.ds(pl.multiple_of(index * 128, 128), 128)
            c = tuple(speeds[k : k + 1, lanes] for k in range(3))

            @pl.when(distance == 0)
            def _():
                center = own[0, :, :, lanes]
                value = step(center, ghost(center, c, 29, lanes), c, 0)
                mid[...] = value
                side_mid[...] = ghost(value, c, 30, lanes)

            @pl.when(distance > 0)
            def _():
                mid[...] = step(own[0, :, :, lanes], up1[:, :, lanes], c, 0)

            @pl.when(distance == 1)
            def _():
                center = up1[:, :, lanes]
                side_mid[...] = step(center, ghost(center, c, 29, lanes), c, 1)

            @pl.when(distance > 1)
            def _():
                side_mid[...] = step(up1[:, :, lanes], up2[:, :, lanes], c, 1)

            out[0, :, :, lanes] = step(mid[...], side_mid[...], c, 2)
            return carry

        lax.fori_loop(0, out.shape[3] // 128, tile, 0)

    @pl.when(block < half_blocks)
    def _():
        half(1, east1, east2)

    @pl.when(block >= half_blocks)
    def _():
        half(0, west1, west2)


def passed_along(value, axis, steps):
    count = lax.axis_size(axis)
    leading, last = (max(0, -steps), min(count, count - steps))
    return lax.ppermute(value, axis, [(source, source + steps) for source in range(leading, last)])


def body(distribution, inflow, wall_temp, face_type):
    slabs, rows, depth, local = distribution.shape
    cells = rows * depth
    halves = local // 2
    layer = NVY * NVZ
    group = min(halves, layer)
    vel = lax.axis_index("vel")
    across, along, along_x, single, collect = tables()

    positive = distribution[0, :, :, halves:]
    negative = distribution[0, :, :, :halves]
    west1 = passed_along(positive, "space", 1)
    east1 = passed_along(negative, "space", -1)
    west2 = passed_along(positive, "space", 2)
    east2 = passed_along(negative, "space", -2)

    ranked = vel * halves + jnp.arange(local, dtype=jnp.int32) % halves
    sign = jnp.where(jnp.arange(local) < halves, -1.0, 1.0)
    speed_x = sign * ((ranked // layer).astype(jnp.float32) + 0.5) * (2.0 * TOP / NVX)
    speed_y = (((ranked % layer) // NVZ).astype(jnp.float32) + 0.5) * (2.0 * TOP / NVY) - TOP
    speed_z = ((ranked % NVZ).astype(jnp.float32) + 0.5) * (2.0 * TOP / NVZ) - TOP
    speeds = jnp.stack([speed_x, speed_y, speed_z] + [jnp.zeros_like(speed_x)] * 5)

    shape = functools.partial(jax.ShapeDtypeStruct, dtype=jnp.float32)
    big = pltpu.CompilerParams(vmem_limit_bytes=48 * 1024 * 1024)
    picked = [[index for _, index in X_BLOCKS[side]] for side in (0, 1)]
    half_groups = halves // group
    level = (vel * halves + jnp.arange(half_groups, dtype=jnp.int32) * group) // layer
    level = jnp.concatenate([NVX // 2 - 1 - level, NVX // 2 + level])
    table = lax.dynamic_slice_in_dim(jnp.asarray(across), vel * halves % layer, group, 1)
    count = table.shape[0]
    slots = len(picked[0]) * ROWS
    sums, inflow_x = pl.pallas_call(
        functools.partial(moment_kernel, half_groups, "space"),
        grid_spec=pltpu.PrefetchScalarGridSpec(
            num_scalar_prefetch=1,
            grid=(2 * half_groups,),
            in_specs=[
                pl.BlockSpec((1, rows, depth, group), lambda i, lv: (0, 0, 0, i)),
                pl.BlockSpec(
                    (1, rows, depth, group), lambda i, lv: (jnp.where(i < half_groups, 1, 0), 0, 0, i)
                ),
                pl.BlockSpec((count, group), lambda i, lv: (0, 0)),
                pl.BlockSpec((1, len(BLOCKS2) * ROWS, count), lambda i, lv: (lv[i], 0, 0)),
                pl.BlockSpec((1, slots, count), lambda i, lv: (lv[i], 0, 0)),
            ],
            out_specs=[
                pl.BlockSpec((len(BLOCKS2) * ROWS, cells), lambda i, lv: (0, 0)),
                pl.BlockSpec((slots, cells), lambda i, lv: (0, 0)),
            ],
        ),
        out_shape=(shape((len(BLOCKS2) * ROWS, cells)), shape((slots, cells))),
        compiler_params=big,
        name="input_moments",
    )(level, distribution, inflow, table, jnp.asarray(along), jnp.asarray(along_x))
    sums, inflow_x = lax.psum((sums, inflow_x), "vel")
    sums = sums.reshape(len(BLOCKS2), ROWS, cells)
    inflow_x = inflow_x.reshape(len(picked[0]), ROWS, cells)
    to_east = jnp.stack([sums[k] for k in picked[0]])
    to_west = jnp.stack([sums[k] for k in picked[1]])
    spread = lax.all_gather(jnp.concatenate([to_east, to_west]).reshape(-1, cells), "space")
    place, count_space = lax.axis_index("space"), lax.axis_size("space")
    spread = spread.reshape(count_space, 2, len(picked[0]), ROWS, cells)
    from_west = lax.dynamic_index_in_dim(spread[:, 0], jnp.maximum(place - 1, 0), 0, False)
    from_east = lax.dynamic_index_in_dim(spread[:, 1], jnp.minimum(place + 1, count_space - 1), 0, False)

    wall_flat = wall_temp.reshape(2, cells)
    kind_flat = face_type.reshape(2, cells)
    spans = [[BLOCKS2[k] for k in picked[side]] for side in (0, 1)]
    speeds_np = [levels(NVX), levels(NVY), levels(NVZ)]
    single_x = np.zeros((2, 3, len(picked[0]) * MONOS, NVX), np.float32)
    for side in (0, 1):
        for index, block in enumerate(spans[side]):
            mono_row = 0
            for monos in MOMENTS:
                for mono in monos:
                    for axis in range(3):
                        single_x[side, axis, index * MONOS + mono_row] = factor(
                            speeds_np[axis], mono[axis], axis_sides(block, axis)
                        )
                    mono_row += 1

    west_pack, east_pack, after, ghosts = pl.pallas_call(
        functools.partial(chain1_kernel, "space", depth),
        out_shape=(
            shape((2 * ROWS, cells)),
            shape((2 * ROWS, cells)),
            shape((len(BLOCKS1), ROWS, cells)),
            shape((2, ROWS, cells)),
        ),
        compiler_params=big,
        name="first_moments",
    )(
        sums, from_west, from_east, inflow_x, wall_flat, kind_flat,
        jnp.asarray(single), jnp.asarray(single_x), jnp.asarray(collect),
    )
    west_in = passed_along(west_pack, "space", 1)
    east_in = passed_along(east_pack, "space", -1)
    fields2, params = pl.pallas_call(
        functools.partial(chain2_kernel, "space", depth),
        out_shape=(shape((ROWS, cells)), shape((2, cells, COLUMNS))),
        compiler_params=big,
        name="second_moments",
    )(
        west_pack, after, west_in, east_in, ghosts, wall_flat, kind_flat,
        jnp.asarray(single), jnp.asarray(collect),
    )
    params = params.reshape(2, rows, depth, COLUMNS)

    width = min(512, halves)
    half_blocks = halves // width
    low = lambda i: (0, 0, jnp.minimum(i, half_blocks - 1))
    high = lambda i: (0, 0, jnp.maximum(i - half_blocks, 0))
    plane = (rows, depth, width)
    updated = pl.pallas_call(
        functools.partial(cell_kernel, "space", half_blocks),
        grid=(2 * half_blocks,),
        in_specs=[
            pl.BlockSpec((1,) + plane, lambda i: (0, 0, 0, i)),
            pl.BlockSpec(plane, high),
            pl.BlockSpec(plane, low),
            pl.BlockSpec(plane, high),
            pl.BlockSpec(plane, low),
            pl.BlockSpec((1,) + plane, lambda i: (jnp.where(i < half_blocks, 1, 0), 0, 0, i)),
            pl.BlockSpec((8, width), lambda i: (0, i)),
            pl.BlockSpec((2, rows, depth, COLUMNS), lambda i: (0, 0, 0, 0)),
        ],
        out_specs=pl.BlockSpec((1,) + plane, lambda i: (0, 0, 0, i)),
        out_shape=shape(distribution.shape),
        scratch_shapes=[
            pltpu.VMEM((31, rows, depth, 128), jnp.float32),
            pltpu.VMEM((3, rows, depth, 128), jnp.float32),
            pltpu.VMEM((3, rows, depth, 128), jnp.float32),
            pltpu.VMEM((rows, depth, 128), jnp.float32),
            pltpu.VMEM((rows, depth, 128), jnp.float32),
        ],
        compiler_params=big,
        name="two_steps",
    )(distribution, west1, east1, west2, east2, inflow, speeds, params)
    fields = fields2[:8].reshape(8, 1, rows, depth)
    return updated, fields


def solution(mesh):
    in_specs = (P("space", None, None, "vel"), P(None, None, None, "vel"), P(), P())
    out_specs = (P("space", None, None, "vel"), P(None, "space", None, None))
    return jax.shard_map(body, mesh=mesh, in_specs=in_specs, out_specs=out_specs, check_vma=False)
```

```python
import functools
import math

import jax
import jax.numpy as jnp
import numpy as np
from jax import lax
from jax.experimental import pallas as pl
from jax.experimental.pallas import tpu as pltpu
from jax.sharding import PartitionSpec as P

NVX = 32
NVY = 32
NVZ = 32
OUTER = 2
INNER = 3

BOX = 512.0
TOP = 4.0
COURANT = 0.08
RATE = 0.8
SHAKHOV = 1.0 / 3.0
HIGHEST = lax.Precision.HIGHEST

MOMENTS = [
    [(0, 0, 0)],
    [(1, 0, 0)],
    [(0, 1, 0)],
    [(0, 0, 1)],
    [(2, 0, 0)],
    [(0, 2, 0)],
    [(0, 0, 2)],
    [(1, 1, 0)],
    [(1, 0, 1)],
    [(0, 1, 1)],
    [(3, 0, 0), (1, 2, 0), (1, 0, 2)],
    [(2, 1, 0), (0, 3, 0), (0, 1, 2)],
    [(2, 0, 1), (0, 2, 1), (0, 0, 3)],
]
ROWS = 16
COLUMNS = 32
MONOS = 24
SIDES = range(6)


def joined(block, side):
    if any(other // 2 == side // 2 and other != side for other in block):
        return None
    return tuple(sorted(block + (side,)))


BLOCKS1 = [()] + [(side,) for side in SIDES]
BLOCKS2 = list(BLOCKS1)
for _block in BLOCKS1[1:]:
    for _side in SIDES:
        _both = joined(_block, _side)
        if _both is not None and _both not in BLOCKS2:
            BLOCKS2.append(_both)
PLACE = {block: index for index, block in enumerate(BLOCKS2)}
X_BLOCKS = [
    [(first, PLACE[joined(block, side)]) for first, block in enumerate(BLOCKS1) if joined(block, side)]
    for side in (0, 1)
]


def levels(count):
    return (np.arange(count) + 0.5) * (2.0 * TOP / count) - TOP


def factor(values, power, sides):
    result = values**power
    for side in sides:
        result = result * np.maximum(values if side % 2 == 0 else -values, 0.0)
    return result


def axis_sides(block, axis):
    return tuple(side for side in block if side // 2 == axis)


@functools.cache
def tables():
    speeds = [levels(NVX), levels(NVY), levels(NVZ)]
    pairs = {}
    entries = []
    for index, block in enumerate(BLOCKS2):
        for row, monos in enumerate(MOMENTS):
            for mono in monos:
                key = (mono[1], axis_sides(block, 1), mono[2], axis_sides(block, 2))
                place = pairs.setdefault(key, len(pairs))
                entries.append((index * ROWS + row, place, mono[0], axis_sides(block, 0)))
    count = -(-len(pairs) // 8) * 8
    across = np.zeros((count, NVY * NVZ), np.float32)
    for (power_y, sides_y, power_z, sides_z), place in pairs.items():
        product = factor(speeds[1], power_y, sides_y)[:, None] * factor(speeds[2], power_z, sides_z)[None]
        across[place] = product.reshape(-1)
    along = np.zeros((NVX, len(BLOCKS2) * ROWS, count), np.float32)
    for row, place, power, sides in entries:
        along[:, row, place] += factor(speeds[0], power, sides)
    along_x = np.zeros((NVX, len(X_BLOCKS[0]) * ROWS, count), np.float32)
    for level in range(NVX):
        side = 0 if level >= NVX // 2 else 1
        for slot, (_, index) in enumerate(X_BLOCKS[side]):
            along_x[level, slot * ROWS : (slot + 1) * ROWS] = along[level, index * ROWS : (index + 1) * ROWS]
    single = np.zeros((3, len(BLOCKS1) * MONOS, NVX), np.float32)
    collect = np.zeros((ROWS, MONOS), np.float32)
    for index, block in enumerate(BLOCKS1):
        mono_row = 0
        for row, monos in enumerate(MOMENTS):
            for mono in monos:
                for axis in range(3):
                    single[axis, index * MONOS + mono_row] = factor(
                        speeds[axis], mono[axis], axis_sides(block, axis)
                    )
                collect[row, mono_row] = 1.0
                mono_row += 1
    return across, along, along_x, single, collect


def shift(value, places):
    size = value.shape[-1]
    return pltpu.roll(value, places % size, value.ndim - 1)


def upwind(value, side, depth):
    step = 1 if side % 2 == 0 else -1
    if side // 2 == 1:
        return shift(value, step * depth)
    cell = lax.broadcasted_iota(jnp.int32, value.shape, value.ndim - 1) % depth
    edge = cell == (0 if step == 1 else depth - 1)
    return jnp.where(edge, shift(value, step - step * depth), shift(value, step))


def macro(moments):
    m = [moments[row : row + 1] * (1.0 / (NVX * NVY * NVZ)) for row in range(13)]
    density = m[0]
    u = [m[1] / density, m[2] / density, m[3] / density]
    energy = m[4] + m[5] + m[6]
    u_sq = u[0] * u[0] + u[1] * u[1] + u[2] * u[2]
    temp = (energy - density * u_sq) / (3.0 * density)
    second = [[m[4], m[7], m[8]], [m[7], m[5], m[9]], [m[8], m[9], m[6]]]
    q = []
    for a in range(3):
        cross = u[0] * second[a][0] + u[1] * second[a][1] + u[2] * second[a][2]
        q.append(0.5 * (m[10 + a] - 2.0 * cross - u[a] * energy + 2.0 * density * u_sq * u[a]))
    rate = RATE * density * jnp.exp(0.19 * jnp.log(temp))
    return density, u, temp, q, rate


def equilibrium_moments(density, u, temp, q, single, collect, blocks):
    rows = blocks * MONOS
    sums = []
    for axis in range(3):
        count = (NVX, NVY, NVZ)[axis]
        cells = density.shape[-1]
        level = lax.broadcasted_iota(jnp.int32, (count, cells), 0).astype(jnp.float32)
        offset = (level + 0.5) * (2.0 * TOP / count) - TOP - u[axis]
        weight = jnp.exp(-offset * offset / (2.0 * temp))
        powers = []
        for power in range(4 if q is not None else 1):
            powers.append(
                jnp.dot(
                    single[axis, :rows], weight, precision=HIGHEST, preferred_element_type=jnp.float32
                )
            )
            weight = weight * offset
        sums.append(powers)
    total = sums[0][0] * sums[1][0] * sums[2][0]
    if q is not None:
        tail = SHAKHOV / (5.0 * density * temp * temp)
        inverse = 1.0 / temp
        extra = 0.0
        for a in range(3):
            b, c = (a + 1) % 3, (a + 2) % 3
            fa, fb, fc = sums[a], sums[b], sums[c]
            term = (fa[3] * inverse - 5.0 * fa[1]) * (fb[0] * fc[0])
            term = term + fa[1] * inverse * (fb[2] * fc[0] + fb[0] * fc[2])
            extra = extra + (q[a] * tail) * term
        total = total + extra
    turn = 2.0 * math.pi * temp
    total = total * (density * BOX / (turn * jnp.sqrt(turn)))
    return [
        jnp.dot(
            collect[...],
            total[index * MONOS : (index + 1) * MONOS],
            precision=HIGHEST,
            preferred_element_type=jnp.float32,
        )
        for index in range(blocks)
    ]


def iterate(moments, single, collect):
    current = moments
    for turn in range(INNER):
        fields = macro(current)
        if turn < INNER - 1:
            (target,) = equilibrium_moments(*fields[:4], single, collect, 1)
            current = (moments + fields[4] * target) / (1.0 + fields[4])
    return fields


def ghost_block(wall, inflow, edge, kind):
    return jnp.where(kind == 0, wall, jnp.where(kind == 1, inflow, edge))


def stack_fields(fields):
    density, u, temp, q, rate = fields
    rows = [density, *u, temp, *q, rate]
    return jnp.concatenate(rows + [jnp.zeros_like(density)] * (ROWS - len(rows)), 0)


def chain1_kernel(axis_name, depth, sums, west, east, inflow, wall_temp, kind, single, single_x, collect,
                  west_out, east_out, flux_out, first_out):
    place = lax.axis_index(axis_name)
    ends = (place == 0, place == lax.axis_size(axis_name) - 1)
    got = (west, east)
    kinds = [kind[face : face + 1] for face in range(2)]
    walls, entering, ratios = [], [], []
    for face in range(2):
        temp = wall_temp[face : face + 1]
        one = jnp.ones_like(temp)
        zero = jnp.zeros_like(temp)
        wall = equilibrium_moments(one, [zero] * 3, temp, None, single_x.at[face], collect, 6)
        walls.append(wall)
        entering.append(wall[0][0:1])
        ratios.append(sums[2 - face][0:1] / wall[0][0:1])
    read = []
    for first, block in enumerate(BLOCKS1):
        value = sums[first]
        flux = jnp.zeros_like(value)
        for side in SIDES:
            both = joined(block, side)
            if both is None:
                continue
            own = sums[PLACE[both]]
            if side < 2:
                slot = [entry[0] for entry in X_BLOCKS[side]].index(first)
                ghost = ghost_block(ratios[side] * walls[side][slot], inflow[slot], own, kinds[side])
                other = jnp.where(ends[side], ghost, got[side][slot])
            else:
                other = upwind(own, side, depth)
            flux = flux + (own - other)
        read.append(value - COURANT * flux)
    fields = iterate(read[0], single, collect)
    target = equilibrium_moments(*fields[:4], single, collect, len(BLOCKS1))
    rate = fields[4]
    after = [(value + rate * goal) / (1.0 + rate) for value, goal in zip(read, target)]
    stacked = stack_fields(fields)
    scale = []
    for face in range(2):
        temp = wall_temp[face : face + 1]
        turn = 2.0 * math.pi * temp
        norm = BOX / (turn * jnp.sqrt(turn))
        ratio2 = after[2 - face][0:1] / entering[face]
        scale.append((ratios[face] * norm, ratio2 * norm, ratio2))
    packed = jnp.concatenate(
        [stacked[:9], scale[0][0], scale[0][1], scale[1][0], scale[1][1], stacked[13:]], 0
    )
    west_out[...] = jnp.concatenate([packed, after[1]], 0)
    east_out[...] = jnp.concatenate([packed, after[2]], 0)
    for index in range(len(BLOCKS1)):
        flux_out[index] = after[index]
    for face in range(2):
        first_out[face] = ghost_block(
            scale[face][2] * walls[face][0], inflow[0], after[1 + face], kinds[face]
        )


def relax_rows(fields):
    row = lambda k: fields[k : k + 1]
    density, temp, rate = row(0), row(4), row(8)
    turn = 2.0 * math.pi * temp
    keep = 1.0 / (1.0 + rate)
    tail = SHAKHOV / (5.0 * density * temp * temp)
    return [
        row(1),
        row(2),
        row(3),
        1.0 / temp,
        row(5) * tail,
        row(6) * tail,
        row(7) * tail,
        density * BOX / (turn * jnp.sqrt(turn)) * rate * keep,
        keep,
    ]


def chain2_kernel(axis_name, depth, own_pack, after, west, east, ghosts, wall_temp, kind, single, collect,
                  fields_out, params_out):
    place = lax.axis_index(axis_name)
    ends = (place == 0, place == lax.axis_size(axis_name) - 1)
    got = (west, east)
    flux = jnp.zeros_like(after[0])
    for side in SIDES:
        own = after[1 + side]
        if side < 2:
            other = jnp.where(ends[side], ghosts[side], got[side][ROWS:])
        else:
            other = upwind(own, side, depth)
        flux = flux + (own - other)
    fields = stack_fields(iterate(after[0] - COURANT * flux, single, collect))
    fields_out[...] = fields
    mine = own_pack[:ROWS]
    for face in range(2):
        near = got[face][:ROWS]
        k = 9 + 2 * face
        rows = relax_rows(mine) + relax_rows(near) + relax_rows(fields)
        rows += [
            kind[face : face + 1].astype(jnp.float32),
            0.5 / wall_temp[face : face + 1],
            jnp.where(ends[face], mine[k : k + 1], near[k : k + 1]),
            mine[k + 1 : k + 2],
        ]
        rows += [jnp.zeros_like(rows[0])] * (COLUMNS - len(rows))
        params_out[face] = jnp.concatenate(rows, 0).T


def moment_kernel(half_groups, axis_name, level, own, inflow, across, along, along_x, out, out_x):
    group = pl.program_id(0)
    cells = out.shape[1]

    def sums(ref, weight):
        inner = 0.0
        value = ref[0].reshape(cells, ref.shape[3])
        table = across[...]
        value_hi = value.astype(jnp.bfloat16)
        table_hi = table.astype(jnp.bfloat16)
        value_lo = (value - value_hi.astype(jnp.float32)).astype(jnp.bfloat16)
        table_lo = (table - table_hi.astype(jnp.float32)).astype(jnp.bfloat16)
        for left, right in ((table_lo, value_hi), (table_hi, value_lo), (table_hi, value_hi)):
            inner = inner + lax.dot_general(
                left, right, (((1,), (1,)), ((), ())), preferred_element_type=jnp.float32
            )
        return jnp.dot(weight[0], inner, precision=HIGHEST, preferred_element_type=jnp.float32)

    @pl.when(group == 0)
    def _():
        out[...] = jnp.zeros_like(out)
        out_x[...] = jnp.zeros_like(out_x)

    out[...] += sums(own, along)

    @pl.when((group >= half_groups) == (lax.axis_index(axis_name) == 0))
    def _():
        out_x[...] += sums(inflow, along_x)


def transported(center, up, c):
    cx, cy, cz = c
    ax, ay, az = COURANT * jnp.abs(cx), COURANT * jnp.abs(cy), COURANT * jnp.abs(cz)
    rows, depth = center.shape[:2]
    up_y = jnp.where(
        cy > 0.0,
        jnp.concatenate([center[rows - 1 :], center[: rows - 1]], 0),
        jnp.concatenate([center[1:], center[:1]], 0),
    )
    up_z = jnp.where(cz > 0.0, pltpu.roll(center, 1, 1), pltpu.roll(center, depth - 1, 1))
    return center * (1.0 - (ax + ay + az)) + (ax * up + ay * up_y + az * up_z)


def cell_kernel(axis_name, half_blocks, own, west1, east1, west2, east2, inflow, speeds, params, out,
                wide, part_r, part_h, mid, side_mid):
    place = lax.axis_index(axis_name)
    last = lax.axis_size(axis_name) - 1
    block = pl.program_id(0)

    @pl.when(block % half_blocks == 0)
    def _():
        face = jnp.where(block < half_blocks, 1, 0)
        for k in range(31):
            wide[k] = jnp.broadcast_to(params[face, :, :, k : k + 1], wide.shape[1:])

    for turn in range(3):
        base = 9 * turn
        px = speeds[0:1, :128] - wide[base]
        pz = speeds[2:3, :128] - wide[base + 2]
        part_r[turn] = (px * px + pz * pz) * wide[base + 3]
        part_h[turn] = wide[base + 4] * px + wide[base + 6] * pz

    def step(center, up, c, turn):
        base = 9 * turn
        read = transported(center, up, c)
        py = c[1] - wide[base + 1]
        r = part_r[turn] + py * py * wide[base + 3]
        heat = part_h[turn] + py * wide[base + 5]
        goal = wide[base + 7] * jnp.exp(-0.5 * r) * (1.0 + heat * (r - 5.0))
        return read * wide[base + 8] + goal

    def half(face, up1, up2):
        distance = place if face == 0 else last - place

        def ghost(edge, c, scale_column, lanes):
            c_sq = c[0] * c[0] + c[1] * c[1] + c[2] * c[2]
            kind = wide[27]
            wall = wide[scale_column] * jnp.exp(-c_sq * wide[28])
            return jnp.where(kind == 0.0, wall, jnp.where(kind == 1.0, inflow[0, :, :, lanes], edge))

        def tile(index, carry):
            lanes = pl.ds(pl.multiple_of(index * 128, 128), 128)
            c = tuple(speeds[k : k + 1, lanes] for k in range(3))

            @pl.when(distance == 0)
            def _():
                center = own[0, :, :, lanes]
                value = step(center, ghost(center, c, 29, lanes), c, 0)
                mid[...] = value
                side_mid[...] = ghost(value, c, 30, lanes)

            @pl.when(distance > 0)
            def _():
                mid[...] = step(own[0, :, :, lanes], up1[:, :, lanes], c, 0)

            @pl.when(distance == 1)
            def _():
                center = up1[:, :, lanes]
                side_mid[...] = step(center, ghost(center, c, 29, lanes), c, 1)

            @pl.when(distance > 1)
            def _():
                side_mid[...] = step(up1[:, :, lanes], up2[:, :, lanes], c, 1)

            out[0, :, :, lanes] = step(mid[...], side_mid[...], c, 2)
            return carry

        lax.fori_loop(0, out.shape[3] // 128, tile, 0)

    @pl.when(block < half_blocks)
    def _():
        half(1, east1, east2)

    @pl.when(block >= half_blocks)
    def _():
        half(0, west1, west2)


def passed_along(value, axis, steps):
    count = lax.axis_size(axis)
    leading, last = (max(0, -steps), min(count, count - steps))
    return lax.ppermute(value, axis, [(source, source + steps) for source in range(leading, last)])


def body(distribution, inflow, wall_temp, face_type):
    slabs, rows, depth, local = distribution.shape
    cells = rows * depth
    halves = local // 2
    layer = NVY * NVZ
    group = min(halves, layer)
    vel = lax.axis_index("vel")
    across, along, along_x, single, collect = tables()

    positive = distribution[0, :, :, halves:]
    negative = distribution[0, :, :, :halves]
    west1 = passed_along(positive, "space", 1)
    east1 = passed_along(negative, "space", -1)
    west2 = passed_along(positive, "space", 2)
    east2 = passed_along(negative, "space", -2)

    ranked = vel * halves + jnp.arange(local, dtype=jnp.int32) % halves
    sign = jnp.where(jnp.arange(local) < halves, -1.0, 1.0)
    speed_x = sign * ((ranked // layer).astype(jnp.float32) + 0.5) * (2.0 * TOP / NVX)
    speed_y = (((ranked % layer) // NVZ).astype(jnp.float32) + 0.5) * (2.0 * TOP / NVY) - TOP
    speed_z = ((ranked % NVZ).astype(jnp.float32) + 0.5) * (2.0 * TOP / NVZ) - TOP
    speeds = jnp.stack([speed_x, speed_y, speed_z] + [jnp.zeros_like(speed_x)] * 5)

    shape = functools.partial(jax.ShapeDtypeStruct, dtype=jnp.float32)
    big = pltpu.CompilerParams(vmem_limit_bytes=48 * 1024 * 1024)
    picked = [[index for _, index in X_BLOCKS[side]] for side in (0, 1)]
    half_groups = halves // group
    level = (vel * halves + jnp.arange(half_groups, dtype=jnp.int32) * group) // layer
    level = jnp.concatenate([NVX // 2 - 1 - level, NVX // 2 + level])
    table = lax.dynamic_slice_in_dim(jnp.asarray(across), vel * halves % layer, group, 1)
    count = table.shape[0]
    slots = len(picked[0]) * ROWS
    sums, inflow_x = pl.pallas_call(
        functools.partial(moment_kernel, half_groups, "space"),
        grid_spec=pltpu.PrefetchScalarGridSpec(
            num_scalar_prefetch=1,
            grid=(2 * half_groups,),
            in_specs=[
                pl.BlockSpec((1, rows, depth, group), lambda i, lv: (0, 0, 0, i)),
                pl.BlockSpec(
                    (1, rows, depth, group), lambda i, lv: (jnp.where(i < half_groups, 1, 0), 0, 0, i)
                ),
                pl.BlockSpec((count, group), lambda i, lv: (0, 0)),
                pl.BlockSpec((1, len(BLOCKS2) * ROWS, count), lambda i, lv: (lv[i], 0, 0)),
                pl.BlockSpec((1, slots, count), lambda i, lv: (lv[i], 0, 0)),
            ],
            out_specs=[
                pl.BlockSpec((len(BLOCKS2) * ROWS, cells), lambda i, lv: (0, 0)),
                pl.BlockSpec((slots, cells), lambda i, lv: (0, 0)),
            ],
        ),
        out_shape=(shape((len(BLOCKS2) * ROWS, cells)), shape((slots, cells))),
        compiler_params=big,
        name="input_moments",
    )(level, distribution, inflow, table, jnp.asarray(along), jnp.asarray(along_x))
    sums, inflow_x = lax.psum((sums, inflow_x), "vel")
    sums = sums.reshape(len(BLOCKS2), ROWS, cells)
    inflow_x = inflow_x.reshape(len(picked[0]), ROWS, cells)
    to_east = jnp.stack([sums[k] for k in picked[0]])
    to_west = jnp.stack([sums[k] for k in picked[1]])
    from_west = passed_along(to_east, "space", 1)
    from_east = passed_along(to_west, "space", -1)

    wall_flat = wall_temp.reshape(2, cells)
    kind_flat = face_type.reshape(2, cells)
    spans = [[BLOCKS2[k] for k in picked[side]] for side in (0, 1)]
    speeds_np = [levels(NVX), levels(NVY), levels(NVZ)]
    single_x = np.zeros((2, 3, len(picked[0]) * MONOS, NVX), np.float32)
    for side in (0, 1):
        for index, block in enumerate(spans[side]):
            mono_row = 0
            for monos in MOMENTS:
                for mono in monos:
                    for axis in range(3):
                        single_x[side, axis, index * MONOS + mono_row] = factor(
                            speeds_np[axis], mono[axis], axis_sides(block, axis)
                        )
                    mono_row += 1

    west_pack, east_pack, after, ghosts = pl.pallas_call(
        functools.partial(chain1_kernel, "space", depth),
        out_shape=(
            shape((2 * ROWS, cells)),
            shape((2 * ROWS, cells)),
            shape((len(BLOCKS1), ROWS, cells)),
            shape((2, ROWS, cells)),
        ),
        compiler_params=big,
        name="first_moments",
    )(
        sums, from_west, from_east, inflow_x, wall_flat, kind_flat,
        jnp.asarray(single), jnp.asarray(single_x), jnp.asarray(collect),
    )
    west_in = passed_along(west_pack, "space", 1)
    east_in = passed_along(east_pack, "space", -1)
    fields2, params = pl.pallas_call(
        functools.partial(chain2_kernel, "space", depth),
        out_shape=(shape((ROWS, cells)), shape((2, cells, COLUMNS))),
        compiler_params=big,
        name="second_moments",
    )(
        west_pack, after, west_in, east_in, ghosts, wall_flat, kind_flat,
        jnp.asarray(single), jnp.asarray(collect),
    )
    params = params.reshape(2, rows, depth, COLUMNS)

    width = min(512, halves)
    half_blocks = halves // width
    low = lambda i: (0, 0, jnp.minimum(i, half_blocks - 1))
    high = lambda i: (0, 0, jnp.maximum(i - half_blocks, 0))
    plane = (rows, depth, width)
    updated = pl.pallas_call(
        functools.partial(cell_kernel, "space", half_blocks),
        grid=(2 * half_blocks,),
        in_specs=[
            pl.BlockSpec((1,) + plane, lambda i: (0, 0, 0, i)),
            pl.BlockSpec(plane, high),
            pl.BlockSpec(plane, low),
            pl.BlockSpec(plane, high),
            pl.BlockSpec(plane, low),
            pl.BlockSpec((1,) + plane, lambda i: (jnp.where(i < half_blocks, 1, 0), 0, 0, i)),
            pl.BlockSpec((8, width), lambda i: (0, i)),
            pl.BlockSpec((2, rows, depth, COLUMNS), lambda i: (0, 0, 0, 0)),
        ],
        out_specs=pl.BlockSpec((1,) + plane, lambda i: (0, 0, 0, i)),
        out_shape=shape(distribution.shape),
        scratch_shapes=[
            pltpu.VMEM((31, rows, depth, 128), jnp.float32),
            pltpu.VMEM((3, rows, depth, 128), jnp.float32),
            pltpu.VMEM((3, rows, depth, 128), jnp.float32),
            pltpu.VMEM((rows, depth, 128), jnp.float32),
            pltpu.VMEM((rows, depth, 128), jnp.float32),
        ],
        compiler_params=big,
        name="two_steps",
    )(distribution, west1, east1, west2, east2, inflow, speeds, params)
    fields = fields2[:8].reshape(8, 1, rows, depth)
    return updated, fields


def solution(mesh):
    in_specs = (P("space", None, None, "vel"), P(None, None, None, "vel"), P(), P())
    out_specs = (P("space", None, None, "vel"), P(None, "space", None, None))
    return jax.shard_map(body, mesh=mesh, in_specs=in_specs, out_specs=out_specs, check_vma=False)
```
